128 devices in a mesh: dp: 16 (over z, y), sub: 8 (over x, core).
Axes of the slice: x: 4, y: 4, z: 4, core: 2. Of those that a mesh axis runs over, the one named last changes fastest.
Arguments:
- embeddings: bfloat16 [262144, 512], P(('dp', 'sub')), may hold values from -6 to 6
- assignment: int32 [262144, 1], P(('dp', 'sub')), may hold values from 0 to 511; in each aligned block of 2048 rows (0 to 2047, 2048 to 4095, ...) at most 8 rows name the same one
- cluster_order: int32 [512], replicated, may hold values from 0 to 511, each once
Outputs:
- centroids: float32 [512, 512], P(('dp', 'sub'))
- row_max: float32 [262144], P(('dp', 'sub'))
- center_cos: float32 [262144], P(('dp', 'sub'))
The draws below stay inside these ranges and needn't reach their ends.
Inputs may be any that keep to these rules, and one draw needn't show every extreme that they name: `assignment`: each cluster is named by at most 8 rows of one device (aligned blocks of 2048 rows), and by exactly 8 in some blocks. `cluster_order`: a permutation of the clusters.
All inputs are finite; a program needn't handle non-finite values.
Results may differ from the reference program's by a relative error of at most 0.0029.
Values may be sent and summed in bfloat16 or wider, within the bound.
No kernel may reach another device: no remote copies, remote signals or barrier semaphores. Data moves between devices by JAX's collectives and lax.ppermute only.
A program may use at most 64 MiB of HBM per device.

```python
import math
import jax
import jax.numpy as jnp
import numpy as np
from jax import lax

D = 512
ROWS_DEV = 2048
CLUSTERS = 512
SLOT = 8
ROWS = 262144
N_DP = 16
N_SUB = 8


def levels(own_key, extent, split, least, high):
    level, own = 1.0, jax.random.fold_in(own_key, 6)
    for axis_at, blocks in split:
        heights = jnp.exp(jax.random.uniform(jax.random.fold_in(own, axis_at), (blocks,), jnp.float32, least / len(split), high / len(split)))
        level = level * jnp.repeat(heights, extent[axis_at] // blocks).reshape([-1 if axis == axis_at else 1 for axis in range(len(extent))])
    return level


def routed_block(rng, own, number, rows, amount, top, limit, skew):
    sequence = jax.random.permutation(rng, amount)
    packed, usual = portions_of(amount, rows * top, limit, skew, True), portions_of(amount, rows * top, limit, skew, False)
    places = jnp.arange(amount)

    def named(tallies, rotation):
        used = int((tallies > 0).sum())
        fixed = max(1, used // 4)
        passed = fixed + (places - fixed + rotation * (used - fixed)) % max(1, amount - fixed)
        return jnp.zeros((amount,), jnp.int32).at[sequence[jnp.where(places < fixed, places, passed)]].set(jnp.asarray(tallies, jnp.int32))

    tallies = jnp.where(number % 4 == 0, named(packed, number // 4), named(usual, number - number // 4 - 1))
    mixed = jax.random.permutation(jax.random.fold_in(own, 3), amount)
    giver, sink = mixed[0:amount // 2 * 2:2], mixed[1:amount // 2 * 2:2]
    room = jnp.minimum(tallies[giver] - 1, limit - tallies[sink]) // 2
    room = jnp.where((giver == sequence[0]) | (sink == sequence[0]) | (tallies[sink] == 0), 0, jnp.maximum(room, 0))
    passed = jax.random.randint(jax.random.fold_in(own, 4), (amount // 2,), 0, 1 << 20) % (room + 1)
    tallies = tallies.at[giver].add(-passed).at[sink].add(passed)
    members = jnp.searchsorted(jnp.cumsum(tallies), jnp.arange(rows * top), side="right").astype(jnp.int32)
    listing = members.reshape(top, rows).T
    listing = listing[jax.random.permutation(jax.random.fold_in(own, 1), rows)]
    rotation = jax.random.randint(jax.random.fold_in(own, 2), (rows, 1), 0, top)
    return jnp.take_along_axis(listing, (jnp.arange(top)[None, :] + rotation) % top, axis=1)


def portions_of(amount, total, bound, skew, full):
    weights = [(1 << 20) // math.isqrt(rank ** skew) + 1 for rank in range(1, amount + 1)]
    largest = bound if full else min(bound, max(-(-total // amount), total * weights[0] // sum(weights)))
    least = 1 if total - largest >= amount - 1 else 0
    holding, spare = [largest] + [least] * (amount - 1), total - largest - least * (amount - 1)
    while spare > 0:
        movable = [i for i in range(1, amount) if holding[i] < largest] or [i for i in range(1, amount) if holding[i] < bound]
        mass, left = sum([weights[i] for i in movable]), spare
        for i in movable:
            more = min(bound - holding[i], max(1, left * weights[i] // mass), spare)
            holding[i] = holding[i] + more
            spare = spare - more
    return np.array(holding)


def centred(own_key, extent, deviation, most, shards=(), held_as=jnp.bfloat16):
    array = deviation * jax.random.normal(own_key, extent, jnp.float32)
    if shards:
        array = array * levels(own_key, extent, shards, -0.22, 0.18)
    return jnp.clip(array, -most, most).astype(held_as)


def setup_inputs(seed: int = 0) -> dict:
    seeds = jax.random.split(jax.random.key(seed), 4)
    embeddings = centred(seeds[0], (ROWS, D), 1.0, 6.0, ((0, 128),))
    assignment_keys = jax.random.split(jax.random.fold_in(seeds[1], 1), ROWS // ROWS_DEV)
    assignment_turns = jax.random.permutation(jax.random.fold_in(seeds[1], 3), ROWS // ROWS_DEV)
    assignment = jax.vmap(lambda own, number: routed_block(jax.random.fold_in(seeds[1], 2), own, number, ROWS_DEV, CLUSTERS, 1, SLOT, 1))(assignment_keys, assignment_turns).reshape((ROWS, 1))
    cluster_order = jax.random.permutation(seeds[2], CLUSTERS).astype(jnp.int32)
    return dict(embeddings=embeddings, assignment=assignment, cluster_order=cluster_order)


def reference(embeddings, assignment, cluster_order):
    floats = embeddings.astype(jnp.float32)
    unit = (floats * lax.rsqrt(lax.optimization_barrier(jnp.sum(floats * floats, axis=1, keepdims=True)) + 1e-06)).astype(jnp.bfloat16)
    unit_f = unit.astype(jnp.float32)
    labels = assignment[:, 0].astype(jnp.int32)
    sums = jax.ops.segment_sum(unit_f, labels, num_segments=CLUSTERS)
    centers = sums * lax.rsqrt(lax.optimization_barrier(jnp.sum(sums * sums, axis=1, keepdims=True)) + 1e-06)
    centroids = centers[cluster_order]
    center_cos = lax.optimization_barrier(jnp.sum(unit_f * centers[labels], axis=1))
    capacity = N_DP * N_SUB * SLOT
    sorter = jnp.argsort(labels, stable=True).astype(jnp.int32)
    sorted_rows = jnp.concatenate([unit_f[sorter], jnp.zeros((capacity, D), jnp.float32)], axis=0)
    counts = jax.ops.segment_sum(jnp.ones((ROWS,), jnp.int32), labels, num_segments=CLUSTERS).astype(jnp.int32)
    starts = (jnp.cumsum(counts) - counts).astype(jnp.int32)
    index = jnp.arange(capacity, dtype=jnp.int32)

    def one_cluster(pair):
        start, count = pair
        block = lax.dynamic_slice_in_dim(sorted_rows, start, capacity, 0)
        gram = jnp.dot(block, block.T, precision=lax.Precision.HIGHEST)
        live = index < count
        mask = live[:, None] & live[None, :] & (index[:, None] != index[None, :])
        return lax.optimization_barrier(jnp.max(jnp.where(mask, gram, jnp.float32(-1.0)), axis=1))
    table = lax.map(one_cluster, (starts, counts))
    sorted_labels = labels[sorter]
    rank_sorted = (jnp.arange(ROWS, dtype=jnp.int32) - starts[sorted_labels]).astype(jnp.int32)
    values = table[sorted_labels, rank_sorted]
    row_max = jnp.zeros((ROWS,), jnp.float32).at[sorter].set(values)
    return (centroids, row_max, center_cos)
```

```python
import functools

import jax
import jax.numpy as jnp
from jax import lax
from jax.experimental import pallas as pl
from jax.experimental.pallas import tpu as pltpu
from jax.sharding import PartitionSpec as P

F32 = jnp.float32
BF16 = jnp.bfloat16
LANES = 128
EMPTY = 2.0
BARRED = -4.0


def place_kernel(slot_size, step_slots, lab_ref, order_ref, emb_ref, out_ref, flat_ref, unit, order_col, counts):
    rows = emb_ref.shape[0]
    clusters = order_ref.shape[1]
    step = pl.program_id(0)
    width = 256

    @pl.when(step == 0)
    def _():
        @pl.loop(0, rows // width)
        def _(b):
            at = pl.ds(pl.multiple_of(b * width, width), width)
            x = emb_ref[at, :].astype(F32)
            ss = jnp.sum(x * x, axis=1, keepdims=True)
            unit[at, :] = (x * lax.rsqrt(ss + 1e-06)).astype(BF16)

        wide = jnp.broadcast_to(order_ref[...].astype(F32), (LANES, clusters))
        order_col[...] = wide.T.astype(jnp.int32)
        s = lax.broadcasted_iota(jnp.int32, (width, width + LANES), 0)
        r = lax.broadcasted_iota(jnp.int32, (width, width + LANES), 1)
        earlier = jnp.where((s < r) | (r >= width), 1.0, 0.0).astype(BF16)
        base = (lax.broadcasted_iota(jnp.int32, (clusters, LANES), 0) * slot_size).astype(F32)
        counts[...] = jnp.zeros_like(counts)
        for b in range(rows // width):
            lab = lab_ref[:, b * width : (b + 1) * width]
            col = order_col[...]
            eq = [col == lab[:, j * LANES : (j + 1) * LANES] for j in range(width // LANES)]
            hot = jnp.concatenate([jnp.where(e, 1.0, 0.0) for e in eq], axis=1).astype(BF16)
            before = jnp.dot(hot, earlier, preferred_element_type=F32)
            carry = counts[...]
            for j in range(width // LANES):
                val = before[:, j * LANES : (j + 1) * LANES] + (carry + base)
                flat = jnp.sum(jnp.where(eq[j], val, 0.0), axis=0, keepdims=True)
                flat_ref[:, b * width + j * LANES : b * width + (j + 1) * LANES] = flat.astype(jnp.int32)
            counts[...] = carry + before[:, width:]

    here = step * step_slots
    ids = here + lax.broadcasted_iota(jnp.int32, (step_slots, rows), 0)
    hits = jnp.where(ids == flat_ref[...], 1.0, 0.0).astype(BF16)
    placed = jnp.dot(hits, unit[...], preferred_element_type=F32)
    groups = step_slots // slot_size
    have = counts[pl.ds(pl.multiple_of(step * groups, groups), groups), :]
    have = jnp.broadcast_to(have[:, None, :], (groups, slot_size, LANES)).reshape(step_slots, LANES)
    rank = lax.rem(lax.broadcasted_iota(jnp.int32, (step_slots, LANES), 0), slot_size).astype(F32)
    first = jnp.where(rank >= have, EMPTY, placed[:, :LANES])
    out_ref[:, :LANES] = first.astype(BF16)
    out_ref[:, LANES:] = placed[:, LANES:].astype(BF16)


def place(labels, order, embeddings, slot_size):
    rows, feats = embeddings.shape
    clusters = order.shape[1]
    slots = clusters * slot_size
    step_slots = 512
    whole = lambda i: (0, 0)
    return pl.pallas_call(
        functools.partial(place_kernel, slot_size, step_slots),
        grid=(slots // step_slots,),
        in_specs=[
            pl.BlockSpec((1, rows), whole),
            pl.BlockSpec((1, clusters), whole),
            pl.BlockSpec((rows, feats), whole),
        ],
        out_specs=[
            pl.BlockSpec((step_slots, feats), lambda i: (i, 0)),
            pl.BlockSpec((1, rows), whole),
        ],
        out_shape=[
            jax.ShapeDtypeStruct((slots, feats), BF16),
            jax.ShapeDtypeStruct((1, rows), jnp.int32),
        ],
        scratch_shapes=[
            pltpu.VMEM((rows, feats), BF16),
            pltpu.VMEM((clusters, LANES), jnp.int32),
            pltpu.VMEM((clusters, LANES), F32),
        ],
        compiler_params=pltpu.CompilerParams(
            dimension_semantics=("arbitrary",), vmem_limit_bytes=32 * 1024 * 1024
        ),
        name="place",
    )(labels, order, embeddings)


def compare_kernel(members, slot_size, in_ref, cent_ref, val_ref, held, pen, sums):
    step = pl.program_id(0)
    rows, feats = in_ref.shape
    sources = rows // (members * slot_size)
    part = sources * slot_size
    per_member = pen.shape[1]
    x = in_ref[...].astype(F32).reshape(sources, members, slot_size, feats)
    at = pl.ds(pl.multiple_of(step * part, part), part)
    for m in range(members):
        first = x[:, m, :, :LANES]
        rest = x[:, m, :, LANES:]
        empty = first > 1.5
        pen[m, at, :] = jnp.where(empty, BARRED, 0.0).reshape(part, LANES)
        first = jnp.where(empty, 0.0, first)
        held[m, at, :LANES] = first.reshape(part, LANES).astype(BF16)
        held[m, at, LANES:] = rest.reshape(part, feats - LANES).astype(BF16)
        total = jnp.concatenate([jnp.sum(first, axis=0), jnp.sum(rest, axis=0)], axis=1)

        @pl.when(step == 0)
        def _():
            sums[m] = total

        @pl.when(step > 0)
        def _():
            sums[m] += total

    @pl.when(step == pl.num_programs(0) - 1)
    def _():
        for m in range(members):
            s = jnp.sum(sums[m], axis=0, keepdims=True)
            center = s * lax.rsqrt(jnp.sum(s * s, axis=1, keepdims=True) + 1e-06)
            cent_ref[m : m + 1, :] = center
            high = center.astype(BF16).astype(F32)
            row = lax.broadcasted_iota(jnp.int32, (16, feats), 0)
            both = jnp.where(row == 0, high, jnp.where(row == 1, center - high, 0.0))
            held[m, per_member : per_member + 16, :] = both.astype(BF16)
        cols = 256
        for m in range(members):
            for j in range(per_member // cols):
                right = held[m, j * cols : (j + 1) * cols, :]
                gram = lax.dot_general(
                    held[m], right, (((1,), (1,)), ((), ())), preferred_element_type=F32
                )
                cosine = gram[per_member : per_member + 1] + gram[per_member + 1 : per_member + 2]
                val_ref[2 * m + 1 : 2 * m + 2, j * cols : (j + 1) * cols] = cosine
                best = jnp.full((1, cols), -1.0, F32)
                for i in range(per_member // cols):
                    block = gram[i * cols : (i + 1) * cols]
                    barred = pen[m, i * cols : (i + 1) * cols, :]
                    block = block + jnp.concatenate([barred] * (cols // LANES), axis=1)
                    if i == j:
                        a = lax.broadcasted_iota(jnp.int32, (cols, cols), 0)
                        b = lax.broadcasted_iota(jnp.int32, (cols, cols), 1)
                        block = jnp.where(a == b, BARRED, block)
                    best = jnp.maximum(best, jnp.max(block, axis=0, keepdims=True))
                val_ref[2 * m : 2 * m + 1, j * cols : (j + 1) * cols] = best


def compare(arrived, members, slot_size):
    slots, feats = arrived.shape
    per_member = slots // members
    step_rows = 512
    whole = lambda i: (0, 0)
    return pl.pallas_call(
        functools.partial(compare_kernel, members, slot_size),
        grid=(slots // step_rows,),
        in_specs=[pl.BlockSpec((step_rows, feats), lambda i: (i, 0))],
        out_specs=[
            pl.BlockSpec((members, feats), whole),
            pl.BlockSpec((2 * members, per_member), whole),
        ],
        out_shape=[
            jax.ShapeDtypeStruct((members, feats), F32),
            jax.ShapeDtypeStruct((2 * members, per_member), F32),
        ],
        scratch_shapes=[
            pltpu.VMEM((members, per_member + 16, feats), BF16),
            pltpu.VMEM((members, per_member, LANES), F32),
            pltpu.VMEM((members, slot_size, feats), F32),
        ],
        compiler_params=pltpu.CompilerParams(
            dimension_semantics=("arbitrary",), vmem_limit_bytes=32 * 1024 * 1024
        ),
        name="compare",
    )(arrived)


def pick_kernel(members, slot_size, back_ref, flat_ref, max_ref, cos_ref):
    owners = back_ref.shape[0]
    rows = flat_ref.shape[1]
    each = 2 * slot_size
    turned = back_ref[...].T
    wide = jnp.concatenate([turned[m * each : (m + 1) * each] for m in range(members)], axis=1)
    high = wide.astype(BF16)
    left = wide - high.astype(F32)
    mid = left.astype(BF16)
    low = (left - mid.astype(F32)).astype(BF16)
    pieces = jnp.concatenate([high, mid, low], axis=0)
    cols = 512
    owner = lax.broadcasted_iota(jnp.int32, (owners, cols), 0) * members
    for b in range(rows // cols):
        at = slice(b * cols, (b + 1) * cols)
        flat = flat_ref[:, at]
        group = lax.div(flat, slot_size)
        rank = lax.rem(flat, slot_size)
        hits = jnp.concatenate(
            [jnp.where(owner == group - m, 1.0, 0.0).astype(BF16) for m in range(members)], axis=0
        )
        got = jnp.dot(pieces, hits, preferred_element_type=F32)
        got = got[:each] + got[each : 2 * each] + got[2 * each :]
        mine = lax.broadcasted_iota(jnp.int32, (slot_size, cols), 0) == rank
        max_ref[:, at] = jnp.sum(jnp.where(mine, got[:slot_size], 0.0), axis=0, keepdims=True)
        cos_ref[:, at] = jnp.sum(jnp.where(mine, got[slot_size:], 0.0), axis=0, keepdims=True)


def pick(back, flat, members, slot_size):
    rows = flat.shape[1]
    return pl.pallas_call(
        functools.partial(pick_kernel, members, slot_size),
        out_shape=[jax.ShapeDtypeStruct((1, rows), F32)] * 2,
        compiler_params=pltpu.CompilerParams(vmem_limit_bytes=32 * 1024 * 1024),
        name="pick",
    )(back, flat)


def on_device(embeddings, assignment, cluster_order):
    devices = lax.axis_size("dp") * lax.axis_size("sub")
    rows, feats = embeddings.shape
    clusters = cluster_order.shape[0]
    members = clusters // devices
    slot_size = 2 * rows // clusters
    both = ("dp", "sub")
    outgoing, flat = place(
        assignment.reshape(1, rows), cluster_order.reshape(1, clusters), embeddings, slot_size
    )
    arrived = lax.all_to_all(
        outgoing.reshape(devices, members * slot_size, feats), both, split_axis=0, concat_axis=0, tiled=True
    )
    centers, values = compare(arrived.reshape(clusters * slot_size, feats), members, slot_size)
    values = jnp.transpose(values.reshape(2 * members, devices, slot_size), (1, 0, 2))
    back = lax.all_to_all(
        values.reshape(devices, 2 * members * slot_size), both, split_axis=0, concat_axis=0, tiled=True
    )
    row_max, center_cos = pick(back, flat, members, slot_size)
    return centers, row_max.reshape(rows), center_cos.reshape(rows)


def solution(mesh):
    return jax.shard_map(
        on_device,
        mesh=mesh,
        in_specs=(P(("dp", "sub"), None), P(("dp", "sub"), None), P()),
        out_specs=(P(("dp", "sub"), None), P(("dp", "sub")), P(("dp", "sub"))),
        check_vma=False,
    )
```

```python
import functools

import jax
import jax.numpy as jnp
from jax import lax
from jax.experimental import pallas as pl
from jax.experimental.pallas import tpu as pltpu
from jax.sharding import PartitionSpec as P

F32 = jnp.float32
BF16 = jnp.bfloat16
LANES = 128
EMPTY = 2.0
BARRED = -4.0


def place_kernel(slot_size, step_slots, lab_hbm, order_hbm, emb_hbm, out_ref, flat_ref, lab_ref, order_ref, emb_ref, unit, sems):
    rows = emb_ref.shape[0]
    clusters = order_ref.shape[1]
    width = 256
    loads = [
        pltpu.make_async_copy(lab_hbm, lab_ref, sems.at[0]),
        pltpu.make_async_copy(order_hbm, order_ref, sems.at[1]),
        pltpu.make_async_copy(emb_hbm, emb_ref, sems.at[2]),
    ]
    for load in loads:
        load.start()
    s = lax.broadcasted_iota(jnp.int32, (width, width + LANES), 0)
    r = lax.broadcasted_iota(jnp.int32, (width, width + LANES), 1)
    earlier = jnp.where((s < r) | (r >= width), 1.0, 0.0).astype(BF16)
    base = (lax.broadcasted_iota(jnp.int32, (clusters, LANES), 0) * slot_size).astype(F32)
    loads[0].wait()
    loads[1].wait()
    wide = jnp.broadcast_to(order_ref[...].astype(F32), (LANES, clusters))
    col = wide.T.astype(jnp.int32)
    carry = jnp.zeros((clusters, LANES), F32)
    for b in range(rows // width):
        lab = lab_ref[:, b * width : (b + 1) * width]
        eq = [col == lab[:, j * LANES : (j + 1) * LANES] for j in range(width // LANES)]
        hot = jnp.concatenate([jnp.where(e, 1.0, 0.0) for e in eq], axis=1).astype(BF16)
        before = jnp.dot(hot, earlier, preferred_element_type=F32)
        for j in range(width // LANES):
            val = before[:, j * LANES : (j + 1) * LANES] + (carry + base)
            flat = jnp.sum(jnp.where(eq[j], val, 0.0), axis=0, keepdims=True)
            flat_ref[:, b * width + j * LANES : b * width + (j + 1) * LANES] = flat.astype(jnp.int32)
        carry = carry + before[:, width:]
    loads[2].wait()
    groups = step_slots // slot_size
    rank = lax.rem(lax.broadcasted_iota(jnp.int32, (step_slots, LANES), 0), slot_size).astype(F32)
    for b in range(rows // width):
        at = slice(b * width, (b + 1) * width)
        x = emb_ref[at, :].astype(F32)
        ss = jnp.sum(x * x, axis=1, keepdims=True)
        unit[at, :] = (x * lax.rsqrt(ss + 1e-06)).astype(BF16)
    for step in range(out_ref.shape[0] // step_slots):
        here = step * step_slots
        ids = here + lax.broadcasted_iota(jnp.int32, (step_slots, rows), 0)
        hits = jnp.where(ids == flat_ref[...], 1.0, 0.0).astype(BF16)
        placed = jnp.dot(hits, unit[...], preferred_element_type=F32)
        have = carry[step * groups : (step + 1) * groups]
        have = jnp.broadcast_to(have[:, None, :], (groups, slot_size, LANES)).reshape(step_slots, LANES)
        first = jnp.where(rank >= have, EMPTY, placed[:, :LANES])
        out_ref[here : here + step_slots, :LANES] = first.astype(BF16)
        out_ref[here : here + step_slots, LANES:] = placed[:, LANES:].astype(BF16)


def place(labels, order, embeddings, slot_size):
    rows, feats = embeddings.shape
    clusters = order.shape[1]
    slots = clusters * slot_size
    step_slots = 1024
    hbm = pl.BlockSpec(memory_space=pltpu.HBM)
    vmem = pl.BlockSpec(memory_space=pltpu.VMEM)
    return pl.pallas_call(
        functools.partial(place_kernel, slot_size, step_slots),
        in_specs=[hbm, hbm, hbm],
        out_specs=[vmem, vmem],
        out_shape=[
            pltpu.VMEM((slots, feats), BF16),
            pltpu.VMEM((1, rows), jnp.int32),
        ],
        scratch_shapes=[
            pltpu.VMEM((1, rows), jnp.int32),
            pltpu.VMEM((1, clusters), jnp.int32),
            pltpu.VMEM((rows, feats), BF16),
            pltpu.VMEM((rows, feats), BF16),
            pltpu.SemaphoreType.DMA((3,)),
        ],
        compiler_params=pltpu.CompilerParams(vmem_limit_bytes=40 * 1024 * 1024),
        name="place",
    )(*(pltpu.with_memory_space_constraint(v, pltpu.HBM) for v in (labels, order, embeddings)))


def compare_kernel(members, slot_size, in_ref, cent_ref, val_ref, held, pen):
    sources, slots, feats = in_ref.shape
    per_member = pen.shape[1]
    batch = 16
    part = batch * slot_size
    cols = 256
    for pair in range(0, members, 2):
        sums = [None, None]
        for g in range(sources // batch):
            x = in_ref[g * batch : (g + 1) * batch, pair * slot_size : (pair + 2) * slot_size, :].astype(F32)
            for h in range(2):
                m = pair + h
                at = slice(g * part, (g + 1) * part)
                first = x[:, h * slot_size : (h + 1) * slot_size, :LANES]
                rest = x[:, h * slot_size : (h + 1) * slot_size, LANES:]
                empty = first > 1.5
                pen[m, at, :] = jnp.where(empty, BARRED, 0.0).reshape(part, LANES)
                first = jnp.where(empty, 0.0, first)
                held[m, at, :LANES] = first.reshape(part, LANES).astype(BF16)
                held[m, at, LANES:] = rest.reshape(part, feats - LANES).astype(BF16)
                total = jnp.concatenate([jnp.sum(first, axis=0), jnp.sum(rest, axis=0)], axis=1)
                sums[h] = total if g == 0 else sums[h] + total
        for h in range(2):
            m = pair + h
            s = jnp.sum(sums[h], axis=0, keepdims=True)
            center = s * lax.rsqrt(jnp.sum(s * s, axis=1, keepdims=True) + 1e-06)
            cent_ref[m : m + 1, :] = center
            high = center.astype(BF16).astype(F32)
            row = lax.broadcasted_iota(jnp.int32, (16, feats), 0)
            both = jnp.where(row == 0, high, jnp.where(row == 1, center - high, 0.0))
            held[m, per_member : per_member + 16, :] = both.astype(BF16)
            for j in range(per_member // cols):
                right = held[m, j * cols : (j + 1) * cols, :]
                gram = lax.dot_general(
                    held[m], right, (((1,), (1,)), ((), ())), preferred_element_type=F32
                )
                cosine = gram[per_member : per_member + 1] + gram[per_member + 1 : per_member + 2]
                val_ref[2 * m + 1 : 2 * m + 2, j * cols : (j + 1) * cols] = cosine
                best = jnp.full((1, cols), -1.0, F32)
                for i in range(per_member // cols):
                    block = gram[i * cols : (i + 1) * cols]
                    barred = pen[m, i * cols : (i + 1) * cols, :]
                    block = block + jnp.concatenate([barred] * (cols // LANES), axis=1)
                    if i == j:
                        a = lax.broadcasted_iota(jnp.int32, (cols, cols), 0)
                        b = lax.broadcasted_iota(jnp.int32, (cols, cols), 1)
                        block = jnp.where(a == b, BARRED, block)
                    best = jnp.maximum(best, jnp.max(block, axis=0, keepdims=True))
                val_ref[2 * m : 2 * m + 1, j * cols : (j + 1) * cols] = best


def compare(arrived, members, slot_size):
    slots, feats = arrived.shape
    per_member = slots // members
    sources = per_member // slot_size
    vmem = pl.BlockSpec(memory_space=pltpu.VMEM)
    return pl.pallas_call(
        functools.partial(compare_kernel, members, slot_size),
        in_specs=[vmem],
        out_specs=[vmem, vmem],
        out_shape=[
            jax.ShapeDtypeStruct((members, feats), F32),
            jax.ShapeDtypeStruct((2 * members, per_member), F32),
        ],
        scratch_shapes=[
            pltpu.VMEM((members, per_member + 16, feats), BF16),
            pltpu.VMEM((members, per_member, LANES), F32),
        ],
        compiler_params=pltpu.CompilerParams(vmem_limit_bytes=40 * 1024 * 1024),
        name="compare",
    )(pltpu.with_memory_space_constraint(arrived.reshape(sources, members * slot_size, feats), pltpu.VMEM))


def pick_kernel(members, slot_size, back_ref, flat_ref, max_ref, cos_ref):
    owners = back_ref.shape[0]
    rows = flat_ref.shape[1]
    each = 2 * slot_size
    turned = back_ref[...].T
    wide = jnp.concatenate([turned[m * each : (m + 1) * each] for m in range(members)], axis=1)
    high = wide.astype(BF16)
    left = wide - high.astype(F32)
    mid = left.astype(BF16)
    low = (left - mid.astype(F32)).astype(BF16)
    pieces = jnp.concatenate([high, mid, low], axis=0)
    cols = 512
    owner = lax.broadcasted_iota(jnp.int32, (owners, cols), 0) * members
    for b in range(rows // cols):
        at = slice(b * cols, (b + 1) * cols)
        flat = flat_ref[:, at]
        group = lax.div(flat, slot_size)
        rank = lax.rem(flat, slot_size)
        hits = jnp.concatenate(
            [jnp.where(owner == group - m, 1.0, 0.0).astype(BF16) for m in range(members)], axis=0
        )
        got = jnp.dot(pieces, hits, preferred_element_type=F32)
        got = got[:each] + got[each : 2 * each] + got[2 * each :]
        mine = lax.broadcasted_iota(jnp.int32, (slot_size, cols), 0) == rank
        max_ref[:, at] = jnp.sum(jnp.where(mine, got[:slot_size], 0.0), axis=0, keepdims=True)
        cos_ref[:, at] = jnp.sum(jnp.where(mine, got[slot_size:], 0.0), axis=0, keepdims=True)


def pick(back, flat, members, slot_size):
    rows = flat.shape[1]
    return pl.pallas_call(
        functools.partial(pick_kernel, members, slot_size),
        out_shape=[jax.ShapeDtypeStruct((1, rows), F32)] * 2,
        compiler_params=pltpu.CompilerParams(vmem_limit_bytes=32 * 1024 * 1024),
        name="pick",
    )(back, flat)


def on_device(embeddings, assignment, cluster_order):
    devices = lax.axis_size("dp") * lax.axis_size("sub")
    rows, feats = embeddings.shape
    clusters = cluster_order.shape[0]
    members = clusters // devices
    slot_size = 2 * rows // clusters
    both = ("dp", "sub")
    outgoing, flat = place(
        assignment.reshape(1, rows), cluster_order.reshape(1, clusters), embeddings, slot_size
    )
    arrived = lax.all_to_all(
        outgoing.reshape(devices, members * slot_size, feats), both, split_axis=0, concat_axis=0, tiled=True
    )
    centers, values = compare(arrived.reshape(clusters * slot_size, feats), members, slot_size)
    values = jnp.transpose(values.reshape(2 * members, devices, slot_size), (1, 0, 2))
    back = lax.all_to_all(
        values.reshape(devices, 2 * members * slot_size), both, split_axis=0, concat_axis=0, tiled=True
    )
    row_max, center_cos = pick(back, flat, members, slot_size)
    return centers, row_max.reshape(rows), center_cos.reshape(rows)


def solution(mesh):
    return jax.shard_map(
        on_device,
        mesh=mesh,
        in_specs=(P(("dp", "sub"), None), P(("dp", "sub"), None), P()),
        out_specs=(P(("dp", "sub"), None), P(("dp", "sub")), P(("dp", "sub"))),
        check_vma=False,
    )
```

```python
import functools

import jax
import jax.numpy as jnp
from jax import lax
from jax.experimental import pallas as pl
from jax.experimental.pallas import tpu as pltpu
from jax.sharding import PartitionSpec as P

F32 = jnp.float32
BF16 = jnp.bfloat16
LANES = 128
EMPTY = 2.0
BARRED = -4.0


def place_kernel(slot_size, step_slots, lab_hbm, order_hbm, emb_hbm, out_ref, flat_ref, lab_ref, order_ref, emb_ref, unit, sems):
    rows = emb_ref.shape[0]
    clusters = order_ref.shape[1]
    width = 256
    loads = [
        pltpu.make_async_copy(lab_hbm, lab_ref, sems.at[0]),
        pltpu.make_async_copy(order_hbm, order_ref, sems.at[1]),
        pltpu.make_async_copy(emb_hbm, emb_ref, sems.at[2]),
    ]
    for load in loads:
        load.start()
    s = lax.broadcasted_iota(jnp.int32, (width, width + LANES), 0)
    r = lax.broadcasted_iota(jnp.int32, (width, width + LANES), 1)
    earlier = jnp.where((s < r) | (r >= width), 1.0, 0.0).astype(BF16)
    base = (lax.broadcasted_iota(jnp.int32, (clusters, LANES), 0) * slot_size).astype(F32)
    loads[0].wait()
    loads[1].wait()
    wide = jnp.broadcast_to(order_ref[...].astype(F32), (LANES, clusters))
    col = wide.T.astype(jnp.int32)
    carry = jnp.zeros((clusters, LANES), F32)
    for b in range(rows // width):
        lab = lab_ref[:, b * width : (b + 1) * width]
        eq = [col == lab[:, j * LANES : (j + 1) * LANES] for j in range(width // LANES)]
        hot = jnp.concatenate([jnp.where(e, 1.0, 0.0) for e in eq], axis=1).astype(BF16)
        before = jnp.dot(hot, earlier, preferred_element_type=F32)
        for j in range(width // LANES):
            val = before[:, j * LANES : (j + 1) * LANES] + (carry + base)
            flat = jnp.sum(jnp.where(eq[j], val, 0.0), axis=0, keepdims=True)
            flat_ref[:, b * width + j * LANES : b * width + (j + 1) * LANES] = flat.astype(jnp.int32)
        carry = carry + before[:, width:]
    loads[2].wait()
    groups = step_slots // slot_size
    rank = lax.rem(lax.broadcasted_iota(jnp.int32, (step_slots, LANES), 0), slot_size).astype(F32)
    for b in range(rows // width):
        at = slice(b * width, (b + 1) * width)
        x = emb_ref[at, :].astype(F32)
        ss = jnp.sum(x * x, axis=1, keepdims=True)
        unit[at, :] = (x * lax.rsqrt(ss + 1e-06)).astype(BF16)
    for step in range(out_ref.shape[0] // step_slots):
        here = step * step_slots
        ids = here + lax.broadcasted_iota(jnp.int32, (step_slots, rows), 0)
        hits = jnp.where(ids == flat_ref[...], 1.0, 0.0).astype(BF16)
        placed = jnp.dot(hits, unit[...], preferred_element_type=F32)
        have = carry[step * groups : (step + 1) * groups]
        have = jnp.broadcast_to(have[:, None, :], (groups, slot_size, LANES)).reshape(step_slots, LANES)
        first = jnp.where(rank >= have, EMPTY, placed[:, :LANES])
        out_ref[here : here + step_slots, :LANES] = first.astype(BF16)
        out_ref[here : here + step_slots, LANES:] = placed[:, LANES:].astype(BF16)


def place(labels, order, embeddings, slot_size):
    rows, feats = embeddings.shape
    clusters = order.shape[1]
    slots = clusters * slot_size
    step_slots = 1024
    hbm = pl.BlockSpec(memory_space=pltpu.HBM)
    vmem = pl.BlockSpec(memory_space=pltpu.VMEM)
    return pl.pallas_call(
        functools.partial(place_kernel, slot_size, step_slots),
        in_specs=[hbm, hbm, hbm],
        out_specs=[vmem, vmem],
        out_shape=[
            pltpu.VMEM((slots, feats), BF16),
            pltpu.VMEM((1, rows), jnp.int32),
        ],
        scratch_shapes=[
            pltpu.VMEM((1, rows), jnp.int32),
            pltpu.VMEM((1, clusters), jnp.int32),
            pltpu.VMEM((rows, feats), BF16),
            pltpu.VMEM((rows, feats), BF16),
            pltpu.SemaphoreType.DMA((3,)),
        ],
        compiler_params=pltpu.CompilerParams(vmem_limit_bytes=40 * 1024 * 1024),
        name="place",
    )(*(pltpu.with_memory_space_constraint(v, pltpu.HBM) for v in (labels, order, embeddings)))


def compare_kernel(members, slot_size, in_ref, cent_ref, val_ref, held, pen):
    sources, slots, feats = in_ref.shape
    per_member = pen.shape[1]
    batch = 16
    part = batch * slot_size
    cols = 256
    for pair in range(0, members, 2):
        sums = [None, None]
        for g in range(sources // batch):
            x = in_ref[g * batch : (g + 1) * batch, pair * slot_size : (pair + 2) * slot_size, :].astype(F32)
            for h in range(2):
                m = pair + h
                at = slice(g * part, (g + 1) * part)
                first = x[:, h * slot_size : (h + 1) * slot_size, :LANES]
                rest = x[:, h * slot_size : (h + 1) * slot_size, LANES:]
                empty = first > 1.5
                pen[m, at, :] = jnp.where(empty, BARRED, 0.0).reshape(part, LANES)
                first = jnp.where(empty, 0.0, first)
                held[m, at, :LANES] = first.reshape(part, LANES).astype(BF16)
                held[m, at, LANES:] = rest.reshape(part, feats - LANES).astype(BF16)
                total = jnp.concatenate([jnp.sum(first, axis=0), jnp.sum(rest, axis=0)], axis=1)
                sums[h] = total if g == 0 else sums[h] + total
        for h in range(2):
            m = pair + h
            s = jnp.sum(sums[h], axis=0, keepdims=True)
            center = s * lax.rsqrt(jnp.sum(s * s, axis=1, keepdims=True) + 1e-06)
            cent_ref[m : m + 1, :] = center
            high = center.astype(BF16).astype(F32)
            row = lax.broadcasted_iota(jnp.int32, (16, feats), 0)
            both = jnp.where(row == 0, high, jnp.where(row == 1, center - high, 0.0))
            held[m, per_member : per_member + 16, :] = both.astype(BF16)
            blocks = per_member // cols
            lane = lax.broadcasted_iota(jnp.int32, (16, LANES), 1)
            pick_lane = jnp.where(lane == 0, 1.0, 0.0).astype(BF16)
            barred_cols = lax.dot_general(
                pick_lane, pen[m].astype(BF16), (((1,), (1,)), ((), ())), preferred_element_type=F32
            )[:1]
            across = [None] * blocks
            for j in range(blocks):
                right = held[m, j * cols : (j + 1) * cols, :]
                gram = lax.dot_general(
                    held[m, j * cols :, :], right, (((1,), (1,)), ((), ())), preferred_element_type=F32
                )
                end = per_member - j * cols
                cosine = gram[end : end + 1] + gram[end + 1 : end + 2]
                val_ref[2 * m + 1 : 2 * m + 2, j * cols : (j + 1) * cols] = cosine
                best = jnp.full((1, cols), -1.0, F32)
                for i in range(j, blocks):
                    block = gram[(i - j) * cols : (i - j + 1) * cols]
                    barred = pen[m, i * cols : (i + 1) * cols, :]
                    down = block + jnp.concatenate([barred] * (cols // LANES), axis=1)
                    if i == j:
                        a = lax.broadcasted_iota(jnp.int32, (cols, cols), 0)
                        b = lax.broadcasted_iota(jnp.int32, (cols, cols), 1)
                        down = jnp.where(a == b, BARRED, down)
                    best = jnp.maximum(best, jnp.max(down, axis=0, keepdims=True))
                    if i > j:
                        side = block + barred_cols[:, j * cols : (j + 1) * cols]
                        for k in range(cols // LANES):
                            piece = side[:, k * LANES : (k + 1) * LANES]
                            across[i] = piece if across[i] is None else jnp.maximum(across[i], piece)
                if across[j] is not None:
                    best = jnp.maximum(best, jnp.max(across[j].T, axis=0, keepdims=True))
                val_ref[2 * m : 2 * m + 1, j * cols : (j + 1) * cols] = best


def compare(arrived, members, slot_size):
    slots, feats = arrived.shape
    per_member = slots // members
    sources = per_member // slot_size
    vmem = pl.BlockSpec(memory_space=pltpu.VMEM)
    return pl.pallas_call(
        functools.partial(compare_kernel, members, slot_size),
        in_specs=[vmem],
        out_specs=[vmem, vmem],
        out_shape=[
            jax.ShapeDtypeStruct((members, feats), F32),
            jax.ShapeDtypeStruct((2 * members, per_member), F32),
        ],
        scratch_shapes=[
            pltpu.VMEM((members, per_member + 16, feats), BF16),
            pltpu.VMEM((members, per_member, LANES), F32),
        ],
        compiler_params=pltpu.CompilerParams(vmem_limit_bytes=40 * 1024 * 1024),
        name="compare",
    )(pltpu.with_memory_space_constraint(arrived.reshape(sources, members * slot_size, feats), pltpu.VMEM))


def pick_kernel(members, slot_size, back_ref, flat_ref, max_ref, cos_ref):
    owners = back_ref.shape[0]
    rows = flat_ref.shape[1]
    each = 2 * slot_size
    turned = back_ref[...].T
    wide = jnp.concatenate([turned[m * each : (m + 1) * each] for m in range(members)], axis=1)
    high = wide.astype(BF16)
    left = wide - high.astype(F32)
    mid = left.astype(BF16)
    low = (left - mid.astype(F32)).astype(BF16)
    pieces = jnp.concatenate([high, mid, low], axis=0)
    cols = 512
    owner = lax.broadcasted_iota(jnp.int32, (owners, cols), 0) * members
    for b in range(rows // cols):
        at = slice(b * cols, (b + 1) * cols)
        flat = flat_ref[:, at]
        group = lax.div(flat, slot_size)
        rank = lax.rem(flat, slot_size)
        hits = jnp.concatenate(
            [jnp.where(owner == group - m, 1.0, 0.0).astype(BF16) for m in range(members)], axis=0
        )
        got = jnp.dot(pieces, hits, preferred_element_type=F32)
        got = got[:each] + got[each : 2 * each] + got[2 * each :]
        mine = lax.broadcasted_iota(jnp.int32, (slot_size, cols), 0) == rank
        max_ref[:, at] = jnp.sum(jnp.where(mine, got[:slot_size], 0.0), axis=0, keepdims=True)
        cos_ref[:, at] = jnp.sum(jnp.where(mine, got[slot_size:], 0.0), axis=0, keepdims=True)


def pick(back, flat, members, slot_size):
    rows = flat.shape[1]
    return pl.pallas_call(
        functools.partial(pick_kernel, members, slot_size),
        out_shape=[jax.ShapeDtypeStruct((1, rows), F32)] * 2,
        compiler_params=pltpu.CompilerParams(vmem_limit_bytes=32 * 1024 * 1024),
        name="pick",
    )(back, flat)


def on_device(embeddings, assignment, cluster_order):
    devices = lax.axis_size("dp") * lax.axis_size("sub")
    rows, feats = embeddings.shape
    clusters = cluster_order.shape[0]
    members = clusters // devices
    slot_size = 2 * rows // clusters
    both = ("dp", "sub")
    outgoing, flat = place(
        assignment.reshape(1, rows), cluster_order.reshape(1, clusters), embeddings, slot_size
    )
    arrived = lax.all_to_all(
        outgoing.reshape(devices, members * slot_size, feats), both, split_axis=0, concat_axis=0, tiled=True
    )
    centers, values = compare(arrived.reshape(clusters * slot_size, feats), members, slot_size)
    values = jnp.transpose(values.reshape(2 * members, devices, slot_size), (1, 0, 2))
    back = lax.all_to_all(
        values.reshape(devices, 2 * members * slot_size), both, split_axis=0, concat_axis=0, tiled=True
    )
    row_max, center_cos = pick(back, flat, members, slot_size)
    return centers, row_max.reshape(rows), center_cos.reshape(rows)


def solution(mesh):
    return jax.shard_map(
        on_device,
        mesh=mesh,
        in_specs=(P(("dp", "sub"), None), P(("dp", "sub"), None), P()),
        out_specs=(P(("dp", "sub"), None), P(("dp", "sub")), P(("dp", "sub"))),
        check_vma=False,
    )
```

```python
import functools

import jax
import jax.numpy as jnp
from jax import lax
from jax.experimental import pallas as pl
from jax.experimental.pallas import tpu as pltpu
from jax.sharding import PartitionSpec as P

F32 = jnp.float32
BF16 = jnp.bfloat16
LANES = 128
EMPTY = 2.0
BARRED = -4.0


def place_kernel(
    slot_size,
    lab_hbm,
    order_hbm,
    emb_hbm,
    out_ref,
    flat_ref,
    lab_ref,
    order_ref,
    emb_ref,
    unit,
    grouped,
    plan_vec,
    plan,
    sems,
):
    rows, feats = emb_ref.shape
    clusters = order_ref.shape[1]
    width = 256
    blocks = rows // width
    parts = grouped.shape[0]
    step_slots = out_ref.shape[0] // parts
    window = step_slots // parts
    loads = [
        pltpu.make_async_copy(lab_hbm, lab_ref, sems.at[0]),
        pltpu.make_async_copy(order_hbm, order_ref, sems.at[1]),
        pltpu.make_async_copy(emb_hbm, emb_ref, sems.at[2]),
    ]
    for load in loads:
        load.start()
    grouped[...] = jnp.zeros_like(grouped)
    s = lax.broadcasted_iota(jnp.int32, (width, width + LANES), 0)
    r = lax.broadcasted_iota(jnp.int32, (width, width + LANES), 1)
    earlier = jnp.where((s < r) | (r >= width), 1.0, 0.0).astype(BF16)
    base = (lax.broadcasted_iota(jnp.int32, (clusters, LANES), 0) * slot_size).astype(F32)
    loads[0].wait()
    loads[1].wait()
    wide = jnp.broadcast_to(order_ref[...].astype(F32), (LANES, clusters))
    col = wide.T.astype(jnp.int32)
    carry = jnp.zeros((clusters, LANES), F32)
    for b in range(blocks):
        lab = lab_ref[:, b * width : (b + 1) * width]
        eq = [col == lab[:, j * LANES : (j + 1) * LANES] for j in range(width // LANES)]
        hot = jnp.concatenate([jnp.where(e, 1.0, 0.0) for e in eq], axis=1).astype(BF16)
        before = jnp.dot(hot, earlier, preferred_element_type=F32)
        for j in range(width // LANES):
            val = before[:, j * LANES : (j + 1) * LANES] + (carry + base)
            flat = jnp.sum(jnp.where(eq[j], val, 0.0), axis=0, keepdims=True)
            flat_ref[:, b * width + j * LANES : b * width + (j + 1) * LANES] = flat.astype(jnp.int32)
        carry = carry + before[:, width:]

    flat_row = flat_ref[...]
    part_row = lax.div(flat_row, step_slots)
    local_row = flat_row - part_row * step_slots
    part_id = lax.broadcasted_iota(jnp.int32, (parts, width), 0)
    inside = [part_id == part_row[:, b * width : (b + 1) * width] for b in range(blocks)]
    hot = jnp.concatenate([jnp.where(e, 1.0, 0.0) for e in inside], axis=0).astype(BF16)
    before = jnp.dot(hot, earlier, preferred_element_type=F32)
    lane = lax.broadcasted_iota(jnp.int32, (parts, LANES), 1)
    start = jnp.zeros((parts, LANES), jnp.int32)
    most = jnp.zeros((parts, LANES), jnp.int32)
    table = jnp.zeros((parts, LANES), jnp.int32)
    target = []
    for b in range(blocks):
        mine = before[b * parts : (b + 1) * parts]
        within = jnp.sum(jnp.where(inside[b], mine[:, :width], 0.0), axis=0, keepdims=True)
        target.append(part_row[:, b * width : (b + 1) * width] * window + within.astype(jnp.int32))
        amount = mine[:, width:].astype(jnp.int32)
        table = jnp.where(lane == b, start, table)
        most = jnp.maximum(most, amount)
        start = start + ((amount + 15) & -16)
    too_far = jnp.max(jnp.where((start > step_slots) | (most > window), 1.0, 0.0), axis=0, keepdims=True)
    table = jnp.where(lane == blocks, jnp.broadcast_to(too_far, (parts, LANES)).astype(jnp.int32), table)
    plan_vec[...] = table
    to_scalars = pltpu.make_async_copy(plan_vec, plan, sems.at[3])
    to_scalars.start()

    upper = lax.broadcasted_iota(jnp.int32, (LANES, width), 0) < LANES // 2
    for b in range(blocks):
        local = local_row[:, b * width : (b + 1) * width]
        group = lax.div(local, slot_size)
        both = jnp.where(upper, group, local - group * slot_size).astype(F32)
        unit[b * width : (b + 1) * width, feats:] = both.T.astype(BF16)
    loads[2].wait()
    for b in range(blocks):
        at = slice(b * width, (b + 1) * width)
        x = emb_ref[at, :].astype(F32)
        ss = jnp.sum(x * x, axis=1, keepdims=True)
        unit[at, :feats] = (x * lax.rsqrt(ss + 1e-06)).astype(BF16)
    to_scalars.wait()
    dense = plan[0, blocks]

    groups = step_slots // slot_size
    rank = lax.rem(lax.broadcasted_iota(jnp.int32, (step_slots, LANES), 0), slot_size).astype(F32)

    def store(part, placed):
        have = carry[part * groups : (part + 1) * groups]
        have = jnp.broadcast_to(have[:, None, :], (groups, slot_size, LANES)).reshape(step_slots, LANES)
        first = jnp.where(rank >= have, EMPTY, placed[:, :LANES])
        at = slice(part * step_slots, (part + 1) * step_slots)
        out_ref[at, :LANES] = first.astype(BF16)
        out_ref[at, LANES:] = placed[:, LANES:].astype(BF16)

    @pl.when(dense == 0)
    def _():
        ids = lax.broadcasted_iota(jnp.int32, (step_slots, width), 0)
        for b in range(blocks):
            hits = jnp.where(ids == target[b], 1.0, 0.0).astype(BF16)
            sorted_rows = jnp.dot(
                hits, unit[b * width : (b + 1) * width, :], preferred_element_type=F32
            ).astype(BF16)
            for part in range(parts):
                at = pl.ds(pl.multiple_of(plan[part, b], 16), window)
                grouped[part, at, :] = sorted_rows[part * window : (part + 1) * window]
        ids = lax.broadcasted_iota(jnp.int32, (step_slots, step_slots), 0)
        for part in range(parts):
            turned = grouped[part, :step_slots, feats:].astype(F32).T
            slot = (turned[:1] * slot_size + turned[LANES // 2 : LANES // 2 + 1]).astype(jnp.int32)
            hits = jnp.where(ids == slot, 1.0, 0.0).astype(BF16)
            store(part, jnp.dot(hits, grouped[part, :step_slots, :feats], preferred_element_type=F32))

    @pl.when(dense != 0)
    def _():
        ids = lax.broadcasted_iota(jnp.int32, (step_slots, rows), 0)
        for part in range(parts):
            hits = jnp.where(ids == flat_ref[...] - part * step_slots, 1.0, 0.0).astype(BF16)
            store(part, jnp.dot(hits, unit[:, :feats], preferred_element_type=F32))


def place(labels, order, embeddings, slot_size):
    rows, feats = embeddings.shape
    clusters = order.shape[1]
    slots = clusters * slot_size
    parts = 8
    step_slots = slots // parts
    hbm = pl.BlockSpec(memory_space=pltpu.HBM)
    vmem = pl.BlockSpec(memory_space=pltpu.VMEM)
    return pl.pallas_call(
        functools.partial(place_kernel, slot_size),
        in_specs=[hbm, hbm, hbm],
        out_specs=[vmem, vmem],
        out_shape=[
            pltpu.VMEM((slots, feats), BF16),
            pltpu.VMEM((1, rows), jnp.int32),
        ],
        scratch_shapes=[
            pltpu.VMEM((1, rows), jnp.int32),
            pltpu.VMEM((1, clusters), jnp.int32),
            pltpu.VMEM((rows, feats), BF16),
            pltpu.VMEM((rows, feats + LANES), BF16),
            pltpu.VMEM((parts, step_slots + step_slots // parts, feats + LANES), BF16),
            pltpu.VMEM((parts, LANES), jnp.int32),
            pltpu.SMEM((parts, LANES), jnp.int32),
            pltpu.SemaphoreType.DMA((4,)),
        ],
        compiler_params=pltpu.CompilerParams(vmem_limit_bytes=44 * 1024 * 1024),
        name="place",
    )(*(pltpu.with_memory_space_constraint(v, pltpu.HBM) for v in (labels, order, embeddings)))


def compare_kernel(members, slot_size, in_ref, cent_ref, val_ref, held, pen):
    sources, slots, feats = in_ref.shape
    per_member = pen.shape[1]
    batch = 16
    part = batch * slot_size
    cols = 256
    for pair in range(0, members, 2):
        sums = [None, None]
        for g in range(sources // batch):
            x = in_ref[g * batch : (g + 1) * batch, pair * slot_size : (pair + 2) * slot_size, :].astype(F32)
            for h in range(2):
                m = pair + h
                at = slice(g * part, (g + 1) * part)
                first = x[:, h * slot_size : (h + 1) * slot_size, :LANES]
                rest = x[:, h * slot_size : (h + 1) * slot_size, LANES:]
                empty = first > 1.5
                pen[m, at, :] = jnp.where(empty, BARRED, 0.0).reshape(part, LANES)
                first = jnp.where(empty, 0.0, first)
                held[m, at, :LANES] = first.reshape(part, LANES).astype(BF16)
                held[m, at, LANES:] = rest.reshape(part, feats - LANES).astype(BF16)
                total = jnp.concatenate([jnp.sum(first, axis=0), jnp.sum(rest, axis=0)], axis=1)
                sums[h] = total if g == 0 else sums[h] + total
        for h in range(2):
            m = pair + h
            s = jnp.sum(sums[h], axis=0, keepdims=True)
            center = s * lax.rsqrt(jnp.sum(s * s, axis=1, keepdims=True) + 1e-06)
            cent_ref[m : m + 1, :] = center
            high = center.astype(BF16).astype(F32)
            row = lax.broadcasted_iota(jnp.int32, (16, feats), 0)
            both = jnp.where(row == 0, high, jnp.where(row == 1, center - high, 0.0))
            held[m, per_member : per_member + 16, :] = both.astype(BF16)
            blocks = per_member // cols
            lane = lax.broadcasted_iota(jnp.int32, (16, LANES), 1)
            pick_lane = jnp.where(lane == 0, 1.0, 0.0).astype(BF16)
            barred_cols = lax.dot_general(
                pick_lane, pen[m].astype(BF16), (((1,), (1,)), ((), ())), preferred_element_type=F32
            )[:1]
            across = [None] * blocks
            for j in range(blocks):
                right = held[m, j * cols : (j + 1) * cols, :]
                gram = lax.dot_general(
                    held[m, j * cols :, :], right, (((1,), (1,)), ((), ())), preferred_element_type=F32
                )
                end = per_member - j * cols
                cosine = gram[end : end + 1] + gram[end + 1 : end + 2]
                val_ref[2 * m + 1 : 2 * m + 2, j * cols : (j + 1) * cols] = cosine
                best = jnp.full((1, cols), -1.0, F32)
                for i in range(j, blocks):
                    block = gram[(i - j) * cols : (i - j + 1) * cols]
                    barred = pen[m, i * cols : (i + 1) * cols, :]
                    down = block + jnp.concatenate([barred] * (cols // LANES), axis=1)
                    if i == j:
                        a = lax.broadcasted_iota(jnp.int32, (cols, cols), 0)
                        b = lax.broadcasted_iota(jnp.int32, (cols, cols), 1)
                        down = jnp.where(a == b, BARRED, down)
                    best = jnp.maximum(best, jnp.max(down, axis=0, keepdims=True))
                    if i > j:
                        side = block + barred_cols[:, j * cols : (j + 1) * cols]
                        for k in range(cols // LANES):
                            piece = side[:, k * LANES : (k + 1) * LANES]
                            across[i] = piece if across[i] is None else jnp.maximum(across[i], piece)
                if across[j] is not None:
                    best = jnp.maximum(best, jnp.max(across[j].T, axis=0, keepdims=True))
                val_ref[2 * m : 2 * m + 1, j * cols : (j + 1) * cols] = best


def compare(arrived, members, slot_size):
    slots, feats = arrived.shape
    per_member = slots // members
    sources = per_member // slot_size
    vmem = pl.BlockSpec(memory_space=pltpu.VMEM)
    return pl.pallas_call(
        functools.partial(compare_kernel, members, slot_size),
        in_specs=[vmem],
        out_specs=[vmem, vmem],
        out_shape=[
            jax.ShapeDtypeStruct((members, feats), F32),
            jax.ShapeDtypeStruct((2 * members, per_member), F32),
        ],
        scratch_shapes=[
            pltpu.VMEM((members, per_member + 16, feats), BF16),
            pltpu.VMEM((members, per_member, LANES), F32),
        ],
        compiler_params=pltpu.CompilerParams(vmem_limit_bytes=40 * 1024 * 1024),
        name="compare",
    )(pltpu.with_memory_space_constraint(arrived.reshape(sources, members * slot_size, feats), pltpu.VMEM))


def pick_kernel(members, slot_size, back_ref, flat_ref, max_ref, cos_ref):
    owners = back_ref.shape[0]
    rows = flat_ref.shape[1]
    each = 2 * slot_size
    turned = back_ref[...].T
    wide = jnp.concatenate([turned[m * each : (m + 1) * each] for m in range(members)], axis=1)
    high = wide.astype(BF16)
    left = wide - high.astype(F32)
    mid = left.astype(BF16)
    low = (left - mid.astype(F32)).astype(BF16)
    pieces = jnp.concatenate([high, mid, low], axis=0)
    cols = 512
    owner = lax.broadcasted_iota(jnp.int32, (owners, cols), 0) * members
    for b in range(rows // cols):
        at = slice(b * cols, (b + 1) * cols)
        flat = flat_ref[:, at]
        group = lax.div(flat, slot_size)
        rank = lax.rem(flat, slot_size)
        hits = jnp.concatenate(
            [jnp.where(owner == group - m, 1.0, 0.0).astype(BF16) for m in range(members)], axis=0
        )
        got = jnp.dot(pieces, hits, preferred_element_type=F32)
        got = got[:each] + got[each : 2 * each] + got[2 * each :]
        mine = lax.broadcasted_iota(jnp.int32, (slot_size, cols), 0) == rank
        max_ref[:, at] = jnp.sum(jnp.where(mine, got[:slot_size], 0.0), axis=0, keepdims=True)
        cos_ref[:, at] = jnp.sum(jnp.where(mine, got[slot_size:], 0.0), axis=0, keepdims=True)


def pick(back, flat, members, slot_size):
    rows = flat.shape[1]
    return pl.pallas_call(
        functools.partial(pick_kernel, members, slot_size),
        out_shape=[jax.ShapeDtypeStruct((1, rows), F32)] * 2,
        compiler_params=pltpu.CompilerParams(vmem_limit_bytes=32 * 1024 * 1024),
        name="pick",
    )(back, flat)


def on_device(embeddings, assignment, cluster_order):
    devices = lax.axis_size("dp") * lax.axis_size("sub")
    rows, feats = embeddings.shape
    clusters = cluster_order.shape[0]
    members = clusters // devices
    slot_size = 2 * rows // clusters
    both = ("dp", "sub")
    outgoing, flat = place(
        assignment.reshape(1, rows), cluster_order.reshape(1, clusters), embeddings, slot_size
    )
    arrived = lax.all_to_all(
        outgoing.reshape(devices, members * slot_size, feats), both, split_axis=0, concat_axis=0, tiled=True
    )
    centers, values = compare(arrived.reshape(clusters * slot_size, feats), members, slot_size)
    values = jnp.transpose(values.reshape(2 * members, devices, slot_size), (1, 0, 2))
    back = lax.all_to_all(
        values.reshape(devices, 2 * members * slot_size), both, split_axis=0, concat_axis=0, tiled=True
    )
    row_max, center_cos = pick(back, flat, members, slot_size)
    return centers, row_max.reshape(rows), center_cos.reshape(rows)


def solution(mesh):
    return jax.shard_map(
        on_device,
        mesh=mesh,
        in_specs=(P(("dp", "sub"), None), P(("dp", "sub"), None), P()),
        out_specs=(P(("dp", "sub"), None), P(("dp", "sub")), P(("dp", "sub"))),
        check_vma=False,
    )
```

```python
import functools

import jax
import jax.numpy as jnp
from jax import lax
from jax.experimental import pallas as pl
from jax.experimental.pallas import tpu as pltpu
from jax.sharding import PartitionSpec as P

F32 = jnp.float32
BF16 = jnp.bfloat16
LANES = 128
EMPTY = 2.0
BARRED = -4.0


def place_kernel(
    slot_size,
    lab_hbm,
    order_hbm,
    emb_hbm,
    out_ref,
    flat_ref,
    lab_ref,
    order_ref,
    emb_ref,
    unit,
    grouped,
    plan_vec,
    plan,
    sems,
):
    rows, feats = emb_ref.shape
    clusters = order_ref.shape[1]
    width = 256
    blocks = rows // width
    parts = grouped.shape[0]
    step_slots = out_ref.shape[0] // parts
    window = step_slots // parts
    loads = [
        pltpu.make_async_copy(lab_hbm, lab_ref, sems.at[0]),
        pltpu.make_async_copy(order_hbm, order_ref, sems.at[1]),
        pltpu.make_async_copy(emb_hbm, emb_ref, sems.at[2]),
    ]
    for load in loads:
        load.start()
    grouped[...] = jnp.zeros_like(grouped)
    s = lax.broadcasted_iota(jnp.int32, (width, width + LANES), 0)
    r = lax.broadcasted_iota(jnp.int32, (width, width + LANES), 1)
    earlier = jnp.where((s < r) | (r >= width), 1.0, 0.0).astype(BF16)
    base = (lax.broadcasted_iota(jnp.int32, (clusters, LANES), 0) * slot_size).astype(F32)
    loads[0].wait()
    loads[1].wait()
    wide = jnp.broadcast_to(order_ref[...].astype(F32), (LANES, clusters))
    col = wide.T.astype(jnp.int32)
    carry = jnp.zeros((clusters, LANES), F32)
    for b in range(blocks):
        lab = lab_ref[:, b * width : (b + 1) * width]
        eq = [col == lab[:, j * LANES : (j + 1) * LANES] for j in range(width // LANES)]
        hot = jnp.concatenate([jnp.where(e, 1.0, 0.0) for e in eq], axis=1).astype(BF16)
        before = jnp.dot(hot, earlier, preferred_element_type=F32)
        for j in range(width // LANES):
            val = before[:, j * LANES : (j + 1) * LANES] + (carry + base)
            flat = jnp.sum(jnp.where(eq[j], val, 0.0), axis=0, keepdims=True)
            flat_ref[:, b * width + j * LANES : b * width + (j + 1) * LANES] = flat.astype(jnp.int32)
        carry = carry + before[:, width:]

    flat_row = flat_ref[...]
    part_row = lax.div(flat_row, step_slots)
    local_row = flat_row - part_row * step_slots
    part_id = lax.broadcasted_iota(jnp.int32, (parts, width), 0)
    inside = [part_id == part_row[:, b * width : (b + 1) * width] for b in range(blocks)]
    hot = jnp.concatenate([jnp.where(e, 1.0, 0.0) for e in inside], axis=0).astype(BF16)
    before = jnp.dot(hot, earlier, preferred_element_type=F32)
    lane = lax.broadcasted_iota(jnp.int32, (parts, LANES), 1)
    start = jnp.zeros((parts, LANES), jnp.int32)
    most = jnp.zeros((parts, LANES), jnp.int32)
    table = jnp.zeros((parts, LANES), jnp.int32)
    target = []
    for b in range(blocks):
        mine = before[b * parts : (b + 1) * parts]
        within = jnp.sum(jnp.where(inside[b], mine[:, :width], 0.0), axis=0, keepdims=True)
        target.append(part_row[:, b * width : (b + 1) * width] * window + within.astype(jnp.int32))
        amount = mine[:, width:].astype(jnp.int32)
        table = jnp.where(lane == b, start, table)
        most = jnp.maximum(most, amount)
        start = start + ((amount + 15) & -16)
    too_far = jnp.max(jnp.where((start > step_slots) | (most > window), 1.0, 0.0), axis=0, keepdims=True)
    table = jnp.where(lane == blocks, jnp.broadcast_to(too_far, (parts, LANES)).astype(jnp.int32), table)
    plan_vec[...] = table
    to_scalars = pltpu.make_async_copy(plan_vec, plan, sems.at[3])
    to_scalars.start()

    upper = lax.broadcasted_iota(jnp.int32, (LANES, width), 0) < LANES // 2
    for b in range(blocks):
        local = local_row[:, b * width : (b + 1) * width]
        group = lax.div(local, slot_size)
        both = jnp.where(upper, group, local - group * slot_size).astype(F32)
        unit[b * width : (b + 1) * width, feats:] = both.T.astype(BF16)
    loads[2].wait()
    for b in range(blocks):
        at = slice(b * width, (b + 1) * width)
        x = emb_ref[at, :].astype(F32)
        ss = jnp.sum(x * x, axis=1, keepdims=True)
        unit[at, :feats] = (x * lax.rsqrt(ss + 1e-06)).astype(BF16)
    to_scalars.wait()
    dense = plan[0, blocks]

    groups = step_slots // slot_size
    rank = lax.rem(lax.broadcasted_iota(jnp.int32, (step_slots, LANES), 0), slot_size).astype(F32)

    def store(part, placed):
        have = carry[part * groups : (part + 1) * groups]
        have = jnp.broadcast_to(have[:, None, :], (groups, slot_size, LANES)).reshape(step_slots, LANES)
        first = jnp.where(rank >= have, EMPTY, placed[:, :LANES])
        at = slice(part * step_slots, (part + 1) * step_slots)
        out_ref[at, :LANES] = first.astype(BF16)
        out_ref[at, LANES:] = placed[:, LANES:].astype(BF16)

    @pl.when(dense == 0)
    def _():
        ids = lax.broadcasted_iota(jnp.int32, (step_slots, width), 0)
        for b in range(blocks):
            hits = jnp.where(ids == target[b], 1.0, 0.0).astype(BF16)
            sorted_rows = jnp.dot(
                hits, unit[b * width : (b + 1) * width, :], preferred_element_type=F32
            ).astype(BF16)
            for part in range(parts):
                at = pl.ds(pl.multiple_of(plan[part, b], 16), window)
                grouped[part, at, :] = sorted_rows[part * window : (part + 1) * window]
        ids = lax.broadcasted_iota(jnp.int32, (step_slots, step_slots), 0)
        for part in range(parts):
            turned = grouped[part, :step_slots, feats:].astype(F32).T
            slot = (turned[:1] * slot_size + turned[LANES // 2 : LANES // 2 + 1]).astype(jnp.int32)
            hits = jnp.where(ids == slot, 1.0, 0.0).astype(BF16)
            store(part, jnp.dot(hits, grouped[part, :step_slots, :feats], preferred_element_type=F32))

    @pl.when(dense != 0)
    def _():
        ids = lax.broadcasted_iota(jnp.int32, (step_slots, rows), 0)
        for part in range(parts):
            hits = jnp.where(ids == flat_ref[...] - part * step_slots, 1.0, 0.0).astype(BF16)
            store(part, jnp.dot(hits, unit[:, :feats], preferred_element_type=F32))


def place(labels, order, embeddings, slot_size):
    rows, feats = embeddings.shape
    clusters = order.shape[1]
    slots = clusters * slot_size
    parts = 8
    step_slots = slots // parts
    hbm = pl.BlockSpec(memory_space=pltpu.HBM)
    vmem = pl.BlockSpec(memory_space=pltpu.VMEM)
    return pl.pallas_call(
        functools.partial(place_kernel, slot_size),
        in_specs=[hbm, hbm, hbm],
        out_specs=[vmem, vmem],
        out_shape=[
            pltpu.VMEM((slots, feats), BF16),
            pltpu.VMEM((1, rows), jnp.int32),
        ],
        scratch_shapes=[
            pltpu.VMEM((1, rows), jnp.int32),
            pltpu.VMEM((1, clusters), jnp.int32),
            pltpu.VMEM((rows, feats), BF16),
            pltpu.VMEM((rows, feats + LANES), BF16),
            pltpu.VMEM((parts, step_slots + step_slots // parts, feats + LANES), BF16),
            pltpu.VMEM((parts, LANES), jnp.int32),
            pltpu.SMEM((parts, LANES), jnp.int32),
            pltpu.SemaphoreType.DMA((4,)),
        ],
        compiler_params=pltpu.CompilerParams(vmem_limit_bytes=44 * 1024 * 1024),
        name="place",
    )(*(pltpu.with_memory_space_constraint(v, pltpu.HBM) for v in (labels, order, embeddings)))


def compare_kernel(members, slot_size, in_ref, cent_ref, back_ref, held, pen, val_ref, turned):
    sources, slots, feats = in_ref.shape
    per_member = pen.shape[1]
    batch = 16
    part = batch * slot_size
    cols = 256
    for pair in range(0, members, 2):
        sums = [None, None]
        for g in range(sources // batch):
            x = in_ref[g * batch : (g + 1) * batch, pair * slot_size : (pair + 2) * slot_size, :].astype(F32)
            for h in range(2):
                m = pair + h
                at = slice(g * part, (g + 1) * part)
                first = x[:, h * slot_size : (h + 1) * slot_size, :LANES]
                rest = x[:, h * slot_size : (h + 1) * slot_size, LANES:]
                empty = first > 1.5
                pen[m, at, :] = jnp.where(empty, BARRED, 0.0).reshape(part, LANES)
                first = jnp.where(empty, 0.0, first)
                held[m, at, :LANES] = first.reshape(part, LANES).astype(BF16)
                held[m, at, LANES:] = rest.reshape(part, feats - LANES).astype(BF16)
                total = jnp.concatenate([jnp.sum(first, axis=0), jnp.sum(rest, axis=0)], axis=1)
                sums[h] = total if g == 0 else sums[h] + total
        for h in range(2):
            m = pair + h
            s = jnp.sum(sums[h], axis=0, keepdims=True)
            center = s * lax.rsqrt(jnp.sum(s * s, axis=1, keepdims=True) + 1e-06)
            cent_ref[m : m + 1, :] = center
            high = center.astype(BF16).astype(F32)
            row = lax.broadcasted_iota(jnp.int32, (16, feats), 0)
            both = jnp.where(row == 0, high, jnp.where(row == 1, center - high, 0.0))
            held[m, per_member : per_member + 16, :] = both.astype(BF16)
            blocks = per_member // cols
            lane = lax.broadcasted_iota(jnp.int32, (16, LANES), 1)
            pick_lane = jnp.where(lane == 0, 1.0, 0.0).astype(BF16)
            barred_cols = lax.dot_general(
                pick_lane, pen[m].astype(BF16), (((1,), (1,)), ((), ())), preferred_element_type=F32
            )[:1]
            across = [None] * blocks
            for j in range(blocks):
                right = held[m, j * cols : (j + 1) * cols, :]
                gram = lax.dot_general(
                    held[m, j * cols :, :], right, (((1,), (1,)), ((), ())), preferred_element_type=F32
                )
                end = per_member - j * cols
                cosine = gram[end : end + 1] + gram[end + 1 : end + 2]
                val_ref[2 * m + 1 : 2 * m + 2, j * cols : (j + 1) * cols] = cosine
                best = jnp.full((1, cols), -1.0, F32)
                for i in range(j, blocks):
                    block = gram[(i - j) * cols : (i - j + 1) * cols]
                    barred = pen[m, i * cols : (i + 1) * cols, :]
                    down = block + jnp.concatenate([barred] * (cols // LANES), axis=1)
                    if i == j:
                        a = lax.broadcasted_iota(jnp.int32, (cols, cols), 0)
                        b = lax.broadcasted_iota(jnp.int32, (cols, cols), 1)
                        down = jnp.where(a == b, BARRED, down)
                    best = jnp.maximum(best, jnp.max(down, axis=0, keepdims=True))
                    if i > j:
                        side = block + barred_cols[:, j * cols : (j + 1) * cols]
                        for k in range(cols // LANES):
                            piece = side[:, k * LANES : (k + 1) * LANES]
                            across[i] = piece if across[i] is None else jnp.maximum(across[i], piece)
                if across[j] is not None:
                    best = jnp.maximum(best, jnp.max(across[j].T, axis=0, keepdims=True))
                val_ref[2 * m : 2 * m + 1, j * cols : (j + 1) * cols] = best

    values = 2 * members
    tiles = per_member // LANES
    stacked = [val_ref[:, i * LANES : (i + 1) * LANES] for i in range(tiles)]
    turned[...] = jnp.concatenate(stacked + [jnp.zeros((LANES - tiles * values, LANES), F32)], axis=0).T
    span = LANES // slot_size
    held_rows = [turned[pl.ds(k, span, stride=slot_size), :] for k in range(slot_size)]
    group = lax.broadcasted_iota(jnp.int32, (span, LANES), 1) // values
    bit = 1
    while bit < slot_size:
        odd = (group & bit) != 0
        for k in range(slot_size):
            if not k & bit:
                low, high = held_rows[k], held_rows[k | bit]
                held_rows[k] = jnp.where(odd, pltpu.roll(high, bit * values, axis=1), low)
                held_rows[k | bit] = jnp.where(odd, high, pltpu.roll(low, LANES - bit * values, axis=1))
        bit *= 2
    for i in range(tiles):
        back_ref[i * span : (i + 1) * span, :] = held_rows[i]


def compare(arrived, members, slot_size):
    slots, feats = arrived.shape
    per_member = slots // members
    sources = per_member // slot_size
    vmem = pl.BlockSpec(memory_space=pltpu.VMEM)
    return pl.pallas_call(
        functools.partial(compare_kernel, members, slot_size),
        in_specs=[vmem],
        out_specs=[vmem, vmem],
        out_shape=[
            jax.ShapeDtypeStruct((members, feats), F32),
            pltpu.VMEM((sources, LANES), F32),
        ],
        scratch_shapes=[
            pltpu.VMEM((members, per_member + 16, feats), BF16),
            pltpu.VMEM((members, per_member, LANES), F32),
            pltpu.VMEM((2 * members, per_member), F32),
            pltpu.VMEM((LANES, LANES), F32),
        ],
        compiler_params=pltpu.CompilerParams(vmem_limit_bytes=40 * 1024 * 1024),
        name="compare",
    )(pltpu.with_memory_space_constraint(arrived.reshape(sources, members * slot_size, feats), pltpu.VMEM))


def pick_kernel(members, slot_size, back_ref, flat_ref, max_ref, cos_ref, turned):
    owners = back_ref.shape[0]
    rows = flat_ref.shape[1]
    each = 2 * slot_size
    turned[...] = back_ref[...].T
    wide = jnp.concatenate(
        [
            jnp.concatenate(
                [turned[pl.ds(2 * m + v, slot_size, stride=2 * members), :] for v in range(2)], axis=0
            )
            for m in range(members)
        ],
        axis=1,
    )
    high = wide.astype(BF16)
    left = wide - high.astype(F32)
    mid = left.astype(BF16)
    low = (left - mid.astype(F32)).astype(BF16)
    pieces = jnp.concatenate([high, mid, low], axis=0)
    cols = 512
    owner = lax.broadcasted_iota(jnp.int32, (owners, cols), 0) * members
    for b in range(rows // cols):
        at = slice(b * cols, (b + 1) * cols)
        flat = flat_ref[:, at]
        group = lax.div(flat, slot_size)
        rank = lax.rem(flat, slot_size)
        hits = jnp.concatenate(
            [jnp.where(owner == group - m, 1.0, 0.0).astype(BF16) for m in range(members)], axis=0
        )
        got = jnp.dot(pieces, hits, preferred_element_type=F32)
        got = got[:each] + got[each : 2 * each] + got[2 * each :]
        mine = lax.broadcasted_iota(jnp.int32, (slot_size, cols), 0) == rank
        max_ref[:, at] = jnp.sum(jnp.where(mine, got[:slot_size], 0.0), axis=0, keepdims=True)
        cos_ref[:, at] = jnp.sum(jnp.where(mine, got[slot_size:], 0.0), axis=0, keepdims=True)


def pick(back, flat, members, slot_size):
    rows = flat.shape[1]
    return pl.pallas_call(
        functools.partial(pick_kernel, members, slot_size),
        out_shape=[jax.ShapeDtypeStruct((1, rows), F32)] * 2,
        scratch_shapes=[pltpu.VMEM((back.shape[1], back.shape[0]), F32)],
        compiler_params=pltpu.CompilerParams(vmem_limit_bytes=32 * 1024 * 1024),
        name="pick",
    )(back, flat)


def on_device(embeddings, assignment, cluster_order):
    devices = lax.axis_size("dp") * lax.axis_size("sub")
    rows, feats = embeddings.shape
    clusters = cluster_order.shape[0]
    members = clusters // devices
    slot_size = 2 * rows // clusters
    both = ("dp", "sub")
    outgoing, flat = place(
        assignment.reshape(1, rows), cluster_order.reshape(1, clusters), embeddings, slot_size
    )
    arrived = lax.all_to_all(
        outgoing.reshape(devices, members * slot_size, feats), both, split_axis=0, concat_axis=0, tiled=True
    )
    centers, values = compare(arrived.reshape(clusters * slot_size, feats), members, slot_size)
    back = lax.all_to_all(
        values.reshape(devices, 1, values.shape[1]), both, split_axis=0, concat_axis=0, tiled=True
    ).reshape(values.shape)
    row_max, center_cos = pick(back, flat, members, slot_size)
    return centers, row_max.reshape(rows), center_cos.reshape(rows)


def solution(mesh):
    return jax.shard_map(
        on_device,
        mesh=mesh,
        in_specs=(P(("dp", "sub"), None), P(("dp", "sub"), None), P()),
        out_specs=(P(("dp", "sub"), None), P(("dp", "sub")), P(("dp", "sub"))),
        check_vma=False,
    )
```

```python
import functools

import jax
import jax.numpy as jnp
from jax import lax
from jax.experimental import pallas as pl
from jax.experimental.pallas import tpu as pltpu
from jax.sharding import PartitionSpec as P

F32 = jnp.float32
BF16 = jnp.bfloat16
LANES = 128
EMPTY = 2.0
BARRED = -4.0


def place_kernel(
    slot_size,
    lab_hbm,
    order_hbm,
    emb_hbm,
    out_ref,
    flat_ref,
    lab_ref,
    order_ref,
    emb_ref,
    unit,
    grouped,
    plan_vec,
    plan,
    sems,
):
    rows, feats = emb_ref.shape
    clusters = order_ref.shape[1]
    width = 256
    blocks = rows // width
    parts = grouped.shape[0]
    step_slots = out_ref.shape[0] // parts
    window = step_slots // parts
    loads = [
        pltpu.make_async_copy(lab_hbm, lab_ref, sems.at[0]),
        pltpu.make_async_copy(order_hbm, order_ref, sems.at[1]),
        pltpu.make_async_copy(emb_hbm, emb_ref, sems.at[2]),
    ]
    for load in loads:
        load.start()
    grouped[...] = jnp.zeros_like(grouped)
    s = lax.broadcasted_iota(jnp.int32, (width, width + LANES), 0)
    r = lax.broadcasted_iota(jnp.int32, (width, width + LANES), 1)
    earlier = jnp.where((s < r) | (r >= width), 1.0, 0.0).astype(BF16)
    base = (lax.broadcasted_iota(jnp.int32, (clusters, LANES), 0) * slot_size).astype(F32)
    loads[0].wait()
    loads[1].wait()
    wide = jnp.broadcast_to(order_ref[...].astype(F32), (LANES, clusters))
    col = wide.T.astype(jnp.int32)
    carry = jnp.zeros((clusters, LANES), F32)
    for b in range(blocks):
        lab = lab_ref[:, b * width : (b + 1) * width]
        eq = [col == lab[:, j * LANES : (j + 1) * LANES] for j in range(width // LANES)]
        hot = jnp.concatenate([jnp.where(e, 1.0, 0.0) for e in eq], axis=1).astype(BF16)
        before = jnp.dot(hot, earlier, preferred_element_type=F32)
        for j in range(width // LANES):
            val = before[:, j * LANES : (j + 1) * LANES] + (carry + base)
            flat = jnp.sum(jnp.where(eq[j], val, 0.0), axis=0, keepdims=True)
            flat_ref[:, b * width + j * LANES : b * width + (j + 1) * LANES] = flat.astype(jnp.int32)
        carry = carry + before[:, width:]

    flat_row = flat_ref[...]
    part_row = lax.div(flat_row, step_slots)
    local_row = flat_row - part_row * step_slots
    part_id = lax.broadcasted_iota(jnp.int32, (parts, width), 0)
    inside = [part_id == part_row[:, b * width : (b + 1) * width] for b in range(blocks)]
    hot = jnp.concatenate([jnp.where(e, 1.0, 0.0) for e in inside], axis=0).astype(BF16)
    before = jnp.dot(hot, earlier, preferred_element_type=F32)
    lane = lax.broadcasted_iota(jnp.int32, (parts, LANES), 1)
    start = jnp.zeros((parts, LANES), jnp.int32)
    most = jnp.zeros((parts, LANES), jnp.int32)
    table = jnp.zeros((parts, LANES), jnp.int32)
    target = []
    for b in range(blocks):
        mine = before[b * parts : (b + 1) * parts]
        within = jnp.sum(jnp.where(inside[b], mine[:, :width], 0.0), axis=0, keepdims=True)
        target.append(part_row[:, b * width : (b + 1) * width] * window + within.astype(jnp.int32))
        amount = mine[:, width:].astype(jnp.int32)
        table = jnp.where(lane == b, start, table)
        most = jnp.maximum(most, amount)
        start = start + ((amount + 15) & -16)
    too_far = jnp.max(jnp.where((start > step_slots) | (most > window), 1.0, 0.0), axis=0, keepdims=True)
    table = jnp.where(lane == blocks, jnp.broadcast_to(too_far, (parts, LANES)).astype(jnp.int32), table)
    plan_vec[...] = table
    to_scalars = pltpu.make_async_copy(plan_vec, plan, sems.at[3])
    to_scalars.start()

    upper = lax.broadcasted_iota(jnp.int32, (LANES, width), 0) < LANES // 2
    for b in range(blocks):
        local = local_row[:, b * width : (b + 1) * width]
        group = lax.div(local, slot_size)
        both = jnp.where(upper, group, local - group * slot_size).astype(F32)
        unit[b * width : (b + 1) * width, feats:] = both.T.astype(BF16)
    loads[2].wait()
    for b in range(blocks):
        at = slice(b * width, (b + 1) * width)
        x = emb_ref[at, :].astype(F32)
        ss = jnp.sum(x * x, axis=1, keepdims=True)
        unit[at, :feats] = (x * lax.rsqrt(ss + 1e-06)).astype(BF16)
    block_ids = lax.broadcasted_iota(jnp.int32, (step_slots, width), 0)

    def sort_block(b):
        hits = jnp.where(block_ids == target[b], 1.0, 0.0).astype(BF16)
        rows_of = unit[b * width : (b + 1) * width, :]
        return jnp.dot(hits, rows_of, preferred_element_type=F32).astype(BF16)

    early = [sort_block(b) for b in range(4)]
    to_scalars.wait()
    dense = plan[0, blocks]

    groups = step_slots // slot_size
    rank = lax.rem(lax.broadcasted_iota(jnp.int32, (step_slots, LANES), 0), slot_size).astype(F32)

    def store(part, placed):
        have = carry[part * groups : (part + 1) * groups]
        have = jnp.broadcast_to(have[:, None, :], (groups, slot_size, LANES)).reshape(step_slots, LANES)
        first = jnp.where(rank >= have, EMPTY, placed[:, :LANES])
        at = slice(part * step_slots, (part + 1) * step_slots)
        out_ref[at, :LANES] = first.astype(BF16)
        out_ref[at, LANES:] = placed[:, LANES:].astype(BF16)

    @pl.when(dense == 0)
    def _():
        for b in range(blocks):
            sorted_rows = early[b] if b < len(early) else sort_block(b)
            for part in range(parts):
                at = pl.ds(pl.multiple_of(plan[part, b], 16), window)
                grouped[part, at, :] = sorted_rows[part * window : (part + 1) * window]
        ids = lax.broadcasted_iota(jnp.int32, (step_slots, step_slots), 0)
        for part in range(parts):
            turned = grouped[part, :step_slots, feats:].astype(F32).T
            slot = (turned[:1] * slot_size + turned[LANES // 2 : LANES // 2 + 1]).astype(jnp.int32)
            hits = jnp.where(ids == slot, 1.0, 0.0).astype(BF16)
            store(part, jnp.dot(hits, grouped[part, :step_slots, :feats], preferred_element_type=F32))

    @pl.when(dense != 0)
    def _():
        ids = lax.broadcasted_iota(jnp.int32, (step_slots, rows), 0)
        for part in range(parts):
            hits = jnp.where(ids == flat_ref[...] - part * step_slots, 1.0, 0.0).astype(BF16)
            store(part, jnp.dot(hits, unit[:, :feats], preferred_element_type=F32))


def place(labels, order, embeddings, slot_size):
    rows, feats = embeddings.shape
    clusters = order.shape[1]
    slots = clusters * slot_size
    parts = 8
    step_slots = slots // parts
    hbm = pl.BlockSpec(memory_space=pltpu.HBM)
    vmem = pl.BlockSpec(memory_space=pltpu.VMEM)
    return pl.pallas_call(
        functools.partial(place_kernel, slot_size),
        in_specs=[hbm, hbm, hbm],
        out_specs=[vmem, vmem],
        out_shape=[
            pltpu.VMEM((slots, feats), BF16),
            pltpu.VMEM((1, rows), jnp.int32),
        ],
        scratch_shapes=[
            pltpu.VMEM((1, rows), jnp.int32),
            pltpu.VMEM((1, clusters), jnp.int32),
            pltpu.VMEM((rows, feats), BF16),
            pltpu.VMEM((rows, feats + LANES), BF16),
            pltpu.VMEM((parts, step_slots + step_slots // parts, feats + LANES), BF16),
            pltpu.VMEM((parts, LANES), jnp.int32),
            pltpu.SMEM((parts, LANES), jnp.int32),
            pltpu.SemaphoreType.DMA((4,)),
        ],
        compiler_params=pltpu.CompilerParams(vmem_limit_bytes=44 * 1024 * 1024),
        name="place",
    )(*(pltpu.with_memory_space_constraint(v, pltpu.HBM) for v in (labels, order, embeddings)))


def compare_kernel(members, slot_size, in_ref, cent_ref, back_ref, held, pen, val_ref, turned):
    sources, slots, feats = in_ref.shape
    per_member = pen.shape[1]
    batch = 8
    part = batch * slot_size
    cols = 256
    for pair in range(0, members, 2):
        sums = [None, None]
        for g in range(sources // batch):
            x = in_ref[g * batch : (g + 1) * batch, pair * slot_size : (pair + 2) * slot_size, :].astype(F32)
            for h in range(2):
                m = pair + h
                at = slice(g * part, (g + 1) * part)
                first = x[:, h * slot_size : (h + 1) * slot_size, :LANES]
                rest = x[:, h * slot_size : (h + 1) * slot_size, LANES:]
                empty = first > 1.5
                pen[m, at, :] = jnp.where(empty, BARRED, 0.0).reshape(part, LANES)
                first = jnp.where(empty, 0.0, first)
                held[m, at, :LANES] = first.reshape(part, LANES).astype(BF16)
                held[m, at, LANES:] = rest.reshape(part, feats - LANES).astype(BF16)
                total = jnp.concatenate([jnp.sum(first, axis=0), jnp.sum(rest, axis=0)], axis=1)
                sums[h] = total if g == 0 else sums[h] + total
        for h in range(2):
            m = pair + h
            s = jnp.sum(sums[h], axis=0, keepdims=True)
            center = s * lax.rsqrt(jnp.sum(s * s, axis=1, keepdims=True) + 1e-06)
            cent_ref[m : m + 1, :] = center
            high = center.astype(BF16).astype(F32)
            row = lax.broadcasted_iota(jnp.int32, (16, feats), 0)
            both = jnp.where(row == 0, high, jnp.where(row == 1, center - high, 0.0))
            held[m, per_member : per_member + 16, :] = both.astype(BF16)
            blocks = per_member // cols
            lane = lax.broadcasted_iota(jnp.int32, (16, LANES), 1)
            pick_lane = jnp.where(lane == 0, 1.0, 0.0).astype(BF16)
            barred_cols = lax.dot_general(
                pick_lane, pen[m].astype(BF16), (((1,), (1,)), ((), ())), preferred_element_type=F32
            )[:1]
            across = [None] * blocks
            for j in range(blocks):
                right = held[m, j * cols : (j + 1) * cols, :]
                gram = lax.dot_general(
                    held[m, j * cols :, :], right, (((1,), (1,)), ((), ())), preferred_element_type=F32
                )
                end = per_member - j * cols
                cosine = gram[end : end + 1] + gram[end + 1 : end + 2]
                val_ref[2 * m + 1 : 2 * m + 2, j * cols : (j + 1) * cols] = cosine
                best = jnp.full((1, cols), -1.0, F32)
                for i in range(j, blocks):
                    block = gram[(i - j) * cols : (i - j + 1) * cols]
                    barred = pen[m, i * cols : (i + 1) * cols, :]
                    down = block + jnp.concatenate([barred] * (cols // LANES), axis=1)
                    if i == j:
                        a = lax.broadcasted_iota(jnp.int32, (cols, cols), 0)
                        b = lax.broadcasted_iota(jnp.int32, (cols, cols), 1)
                        down = jnp.where(a == b, BARRED, down)
                    best = jnp.maximum(best, jnp.max(down, axis=0, keepdims=True))
                    if i > j:
                        side = block + barred_cols[:, j * cols : (j + 1) * cols]
                        for k in range(cols // LANES):
                            piece = side[:, k * LANES : (k + 1) * LANES]
                            across[i] = piece if across[i] is None else jnp.maximum(across[i], piece)
                if across[j] is not None:
                    best = jnp.maximum(best, jnp.max(across[j].T, axis=0, keepdims=True))
                val_ref[2 * m : 2 * m + 1, j * cols : (j + 1) * cols] = best

    values = 2 * members
    tiles = per_member // LANES
    stacked = [val_ref[:, i * LANES : (i + 1) * LANES] for i in range(tiles)]
    turned[...] = jnp.concatenate(stacked + [jnp.zeros((LANES - tiles * values, LANES), F32)], axis=0).T
    span = LANES // slot_size
    held_rows = [turned[pl.ds(k, span, stride=slot_size), :] for k in range(slot_size)]
    group = lax.broadcasted_iota(jnp.int32, (span, LANES), 1) // values
    bit = 1
    while bit < slot_size:
        odd = (group & bit) != 0
        for k in range(slot_size):
            if not k & bit:
                low, high = held_rows[k], held_rows[k | bit]
                held_rows[k] = jnp.where(odd, pltpu.roll(high, bit * values, axis=1), low)
                held_rows[k | bit] = jnp.where(odd, high, pltpu.roll(low, LANES - bit * values, axis=1))
        bit *= 2
    for i in range(tiles):
        back_ref[i * span : (i + 1) * span, :] = held_rows[i]


def compare(arrived, members, slot_size):
    slots, feats = arrived.shape
    per_member = slots // members
    sources = per_member // slot_size
    vmem = pl.BlockSpec(memory_space=pltpu.VMEM)
    return pl.pallas_call(
        functools.partial(compare_kernel, members, slot_size),
        in_specs=[vmem],
        out_specs=[vmem, vmem],
        out_shape=[
            jax.ShapeDtypeStruct((members, feats), F32),
            pltpu.VMEM((sources, LANES), F32),
        ],
        scratch_shapes=[
            pltpu.VMEM((members, per_member + 16, feats), BF16),
            pltpu.VMEM((members, per_member, LANES), F32),
            pltpu.VMEM((2 * members, per_member), F32),
            pltpu.VMEM((LANES, LANES), F32),
        ],
        compiler_params=pltpu.CompilerParams(vmem_limit_bytes=40 * 1024 * 1024),
        name="compare",
    )(pltpu.with_memory_space_constraint(arrived.reshape(sources, members * slot_size, feats), pltpu.VMEM))


def pick_kernel(members, slot_size, back_ref, flat_ref, max_ref, cos_ref, turned):
    owners = back_ref.shape[0]
    rows = flat_ref.shape[1]
    each = 2 * slot_size
    turned[...] = back_ref[...].T
    wide = jnp.concatenate(
        [
            jnp.concatenate(
                [turned[pl.ds(2 * m + v, slot_size, stride=2 * members), :] for v in range(2)], axis=0
            )
            for m in range(members)
        ],
        axis=1,
    )
    high = wide.astype(BF16)
    left = wide - high.astype(F32)
    mid = left.astype(BF16)
    low = (left - mid.astype(F32)).astype(BF16)
    pieces = jnp.concatenate([high, mid, low], axis=0)
    cols = 512
    owner = lax.broadcasted_iota(jnp.int32, (owners, cols), 0) * members
    for b in range(rows // cols):
        at = slice(b * cols, (b + 1) * cols)
        flat = flat_ref[:, at]
        group = lax.div(flat, slot_size)
        rank = lax.rem(flat, slot_size)
        hits = jnp.concatenate(
            [jnp.where(owner == group - m, 1.0, 0.0).astype(BF16) for m in range(members)], axis=0
        )
        got = jnp.dot(pieces, hits, preferred_element_type=F32)
        got = got[:each] + got[each : 2 * each] + got[2 * each :]
        mine = lax.broadcasted_iota(jnp.int32, (slot_size, cols), 0) == rank
        max_ref[:, at] = jnp.sum(jnp.where(mine, got[:slot_size], 0.0), axis=0, keepdims=True)
        cos_ref[:, at] = jnp.sum(jnp.where(mine, got[slot_size:], 0.0), axis=0, keepdims=True)


def pick(back, flat, members, slot_size):
    rows = flat.shape[1]
    return pl.pallas_call(
        functools.partial(pick_kernel, members, slot_size),
        out_shape=[jax.ShapeDtypeStruct((1, rows), F32)] * 2,
        scratch_shapes=[pltpu.VMEM((back.shape[1], back.shape[0]), F32)],
        compiler_params=pltpu.CompilerParams(vmem_limit_bytes=32 * 1024 * 1024),
        name="pick",
    )(back, flat)


def on_device(embeddings, assignment, cluster_order):
    devices = lax.axis_size("dp") * lax.axis_size("sub")
    rows, feats = embeddings.shape
    clusters = cluster_order.shape[0]
    members = clusters // devices
    slot_size = 2 * rows // clusters
    both = ("dp", "sub")
    outgoing, flat = place(
        assignment.reshape(1, rows), cluster_order.reshape(1, clusters), embeddings, slot_size
    )
    arrived = lax.all_to_all(
        outgoing.reshape(devices, members * slot_size, feats), both, split_axis=0, concat_axis=0, tiled=True
    )
    centers, values = compare(arrived.reshape(clusters * slot_size, feats), members, slot_size)
    back = lax.all_to_all(
        values.reshape(devices, 1, values.shape[1]), both, split_axis=0, concat_axis=0, tiled=True
    ).reshape(values.shape)
    row_max, center_cos = pick(back, flat, members, slot_size)
    return centers, row_max.reshape(rows), center_cos.reshape(rows)


def solution(mesh):
    return jax.shard_map(
        on_device,
        mesh=mesh,
        in_specs=(P(("dp", "sub"), None), P(("dp", "sub"), None), P()),
        out_specs=(P(("dp", "sub"), None), P(("dp", "sub")), P(("dp", "sub"))),
        check_vma=False,
    )
```

```python
import functools

import jax
import jax.numpy as jnp
from jax import lax
from jax.experimental import pallas as pl
from jax.experimental.pallas import tpu as pltpu
from jax.sharding import PartitionSpec as P

F32 = jnp.float32
BF16 = jnp.bfloat16
LANES = 128
EMPTY = 2.0
BARRED = -4.0


def place_kernel(
    slot_size,
    lab_hbm,
    order_hbm,
    emb_hbm,
    out_ref,
    flat_ref,
    lab_ref,
    order_ref,
    emb_ref,
    unit,
    grouped,
    plan_vec,
    plan,
    sems,
):
    rows, feats = emb_ref.shape
    clusters = order_ref.shape[1]
    width = 256
    blocks = rows // width
    parts = grouped.shape[0]
    step_slots = out_ref.shape[0] // parts
    window = step_slots // parts
    loads = [
        pltpu.make_async_copy(lab_hbm, lab_ref, sems.at[0]),
        pltpu.make_async_copy(order_hbm, order_ref, sems.at[1]),
        pltpu.make_async_copy(emb_hbm, emb_ref, sems.at[2]),
    ]
    for load in loads:
        load.start()
    grouped[...] = jnp.zeros_like(grouped)
    s = lax.broadcasted_iota(jnp.int32, (width, width + LANES), 0)
    r = lax.broadcasted_iota(jnp.int32, (width, width + LANES), 1)
    earlier = jnp.where((s < r) | (r >= width), 1.0, 0.0).astype(BF16)
    base = (lax.broadcasted_iota(jnp.int32, (clusters, LANES), 0) * slot_size).astype(F32)
    loads[0].wait()
    loads[1].wait()
    wide = jnp.broadcast_to(order_ref[...].astype(F32), (LANES, clusters))
    col = wide.T.astype(jnp.int32)
    carry = jnp.zeros((clusters, LANES), F32)
    for b in range(blocks):
        lab = lab_ref[:, b * width : (b + 1) * width]
        eq = [col == lab[:, j * LANES : (j + 1) * LANES] for j in range(width // LANES)]
        hot = jnp.concatenate([jnp.where(e, 1.0, 0.0) for e in eq], axis=1).astype(BF16)
        before = jnp.dot(hot, earlier, preferred_element_type=F32)
        for j in range(width // LANES):
            val = before[:, j * LANES : (j + 1) * LANES] + (carry + base)
            flat = jnp.sum(jnp.where(eq[j], val, 0.0), axis=0, keepdims=True)
            flat_ref[:, b * width + j * LANES : b * width + (j + 1) * LANES] = flat.astype(jnp.int32)
        carry = carry + before[:, width:]

    flat_row = flat_ref[...]
    part_row = lax.div(flat_row, step_slots)
    local_row = flat_row - part_row * step_slots
    part_id = lax.broadcasted_iota(jnp.int32, (parts, width), 0)
    inside = [part_id == part_row[:, b * width : (b + 1) * width] for b in range(blocks)]
    hot = jnp.concatenate([jnp.where(e, 1.0, 0.0) for e in inside], axis=0).astype(BF16)
    before = jnp.dot(hot, earlier, preferred_element_type=F32)
    lane = lax.broadcasted_iota(jnp.int32, (parts, LANES), 1)
    start = jnp.zeros((parts, LANES), jnp.int32)
    most = jnp.zeros((parts, LANES), jnp.int32)
    table = jnp.zeros((parts, LANES), jnp.int32)
    target = []
    for b in range(blocks):
        mine = before[b * parts : (b + 1) * parts]
        within = jnp.sum(jnp.where(inside[b], mine[:, :width], 0.0), axis=0, keepdims=True)
        target.append(part_row[:, b * width : (b + 1) * width] * window + within.astype(jnp.int32))
        amount = mine[:, width:].astype(jnp.int32)
        table = jnp.where(lane == b, start, table)
        most = jnp.maximum(most, amount)
        start = start + ((amount + 15) & -16)
    too_far = jnp.max(jnp.where((start > step_slots) | (most > window), 1.0, 0.0), axis=0, keepdims=True)
    table = jnp.where(lane == blocks, jnp.broadcast_to(too_far, (parts, LANES)).astype(jnp.int32), table)
    plan_vec[...] = table
    to_scalars = pltpu.make_async_copy(plan_vec, plan, sems.at[3])
    to_scalars.start()

    upper = lax.broadcasted_iota(jnp.int32, (LANES, width), 0) < LANES // 2
    for b in range(blocks):
        local = local_row[:, b * width : (b + 1) * width]
        group = lax.div(local, slot_size)
        both = jnp.where(upper, group, local - group * slot_size).astype(F32)
        unit[b * width : (b + 1) * width, feats:] = both.T.astype(BF16)
    loads[2].wait()
    for b in range(blocks):
        at = slice(b * width, (b + 1) * width)
        x = emb_ref[at, :].astype(F32)
        ss = jnp.sum(x * x, axis=1, keepdims=True)
        unit[at, :feats] = (x * lax.rsqrt(ss + 1e-06)).astype(BF16)
    block_ids = lax.broadcasted_iota(jnp.int32, (step_slots, width), 0)

    def sort_block(b):
        hits = jnp.where(block_ids == target[b], 1.0, 0.0).astype(BF16)
        rows_of = unit[b * width : (b + 1) * width, :]
        return jnp.dot(hits, rows_of, preferred_element_type=F32).astype(BF16)

    early = [sort_block(b) for b in range(4)]
    to_scalars.wait()
    dense = plan[0, blocks]

    groups = step_slots // slot_size
    rank = lax.rem(lax.broadcasted_iota(jnp.int32, (step_slots, LANES), 0), slot_size).astype(F32)

    def store(part, placed):
        have = carry[part * groups : (part + 1) * groups]
        have = jnp.broadcast_to(have[:, None, :], (groups, slot_size, LANES)).reshape(step_slots, LANES)
        first = jnp.where(rank >= have, EMPTY, placed[:, :LANES])
        at = slice(part * step_slots, (part + 1) * step_slots)
        out_ref[at, :LANES] = first.astype(BF16)
        out_ref[at, LANES:] = placed[:, LANES:].astype(BF16)

    @pl.when(dense == 0)
    def _():
        for b in range(blocks):
            sorted_rows = early[b] if b < len(early) else sort_block(b)
            for part in range(parts):
                at = pl.ds(pl.multiple_of(plan[part, b], 16), window)
                grouped[part, at, :] = sorted_rows[part * window : (part + 1) * window]
        ids = lax.broadcasted_iota(jnp.int32, (step_slots, step_slots), 0)
        for part in range(parts):
            turned = grouped[part, :step_slots, feats:].astype(F32).T
            slot = (turned[:1] * slot_size + turned[LANES // 2 : LANES // 2 + 1]).astype(jnp.int32)
            hits = jnp.where(ids == slot, 1.0, 0.0).astype(BF16)
            store(part, jnp.dot(hits, grouped[part, :step_slots, :feats], preferred_element_type=F32))

    @pl.when(dense != 0)
    def _():
        ids = lax.broadcasted_iota(jnp.int32, (step_slots, rows), 0)
        for part in range(parts):
            hits = jnp.where(ids == flat_ref[...] - part * step_slots, 1.0, 0.0).astype(BF16)
            store(part, jnp.dot(hits, unit[:, :feats], preferred_element_type=F32))


def place(labels, order, embeddings, slot_size):
    rows, feats = embeddings.shape
    clusters = order.shape[1]
    slots = clusters * slot_size
    parts = 8
    step_slots = slots // parts
    hbm = pl.BlockSpec(memory_space=pltpu.HBM)
    vmem = pl.BlockSpec(memory_space=pltpu.VMEM)
    return pl.pallas_call(
        functools.partial(place_kernel, slot_size),
        in_specs=[hbm, hbm, hbm],
        out_specs=[vmem, vmem],
        out_shape=[
            pltpu.VMEM((slots, feats), BF16),
            pltpu.VMEM((1, rows), jnp.int32),
        ],
        scratch_shapes=[
            pltpu.VMEM((1, rows), jnp.int32),
            pltpu.VMEM((1, clusters), jnp.int32),
            pltpu.VMEM((rows, feats), BF16),
            pltpu.VMEM((rows, feats + LANES), BF16),
            pltpu.VMEM((parts, step_slots + step_slots // parts, feats + LANES), BF16),
            pltpu.VMEM((parts, LANES), jnp.int32),
            pltpu.SMEM((parts, LANES), jnp.int32),
            pltpu.SemaphoreType.DMA((4,)),
        ],
        compiler_params=pltpu.CompilerParams(vmem_limit_bytes=44 * 1024 * 1024),
        name="place",
    )(*(pltpu.with_memory_space_constraint(v, pltpu.HBM) for v in (labels, order, embeddings)))


def compare_kernel(members, slot_size, in_ref, cent_ref, back_ref, held, pen, val_ref, turned):
    sources, slots, feats = in_ref.shape
    per_member = pen.shape[1]
    batch = 16
    part = batch * slot_size
    cols = 256
    for pair in range(0, members, 2):
        sums = [None, None]
        for g in range(sources // batch):
            x = in_ref[g * batch : (g + 1) * batch, pair * slot_size : (pair + 2) * slot_size, :].astype(F32)
            for h in range(2):
                m = pair + h
                at = slice(g * part, (g + 1) * part)
                first = x[:, h * slot_size : (h + 1) * slot_size, :LANES]
                rest = x[:, h * slot_size : (h + 1) * slot_size, LANES:]
                empty = first > 1.5
                pen[m, at, :] = jnp.where(empty, BARRED, 0.0).reshape(part, LANES)
                first = jnp.where(empty, 0.0, first)
                held[m, at, :LANES] = first.reshape(part, LANES).astype(BF16)
                held[m, at, LANES:] = rest.reshape(part, feats - LANES).astype(BF16)
                total = jnp.concatenate([jnp.sum(first, axis=0), jnp.sum(rest, axis=0)], axis=1)
                sums[h] = total if g == 0 else sums[h] + total
        for h in range(2):
            m = pair + h
            s = jnp.sum(sums[h], axis=0, keepdims=True)
            center = s * lax.rsqrt(jnp.sum(s * s, axis=1, keepdims=True) + 1e-06)
            cent_ref[m : m + 1, :] = center
            high = center.astype(BF16).astype(F32)
            row = lax.broadcasted_iota(jnp.int32, (16, feats), 0)
            both = jnp.where(row == 0, high, jnp.where(row == 1, center - high, 0.0))
            held[m, per_member : per_member + 16, :] = both.astype(BF16)
            blocks = per_member // cols
            lane = lax.broadcasted_iota(jnp.int32, (16, LANES), 1)
            pick_lane = jnp.where(lane == 0, 1.0, 0.0).astype(BF16)
            barred_cols = lax.dot_general(
                pick_lane, pen[m].astype(BF16), (((1,), (1,)), ((), ())), preferred_element_type=F32
            )[:1]
            across = [None] * blocks
            for j in range(blocks):
                right = held[m, j * cols : (j + 1) * cols, :]
                gram = lax.dot_general(
                    held[m, j * cols :, :], right, (((1,), (1,)), ((), ())), preferred_element_type=F32
                )
                end = per_member - j * cols
                cosine = gram[end : end + 1] + gram[end + 1 : end + 2]
                val_ref[2 * m + 1 : 2 * m + 2, j * cols : (j + 1) * cols] = cosine
                best = jnp.full((1, cols), -1.0, F32)
                for i in range(j, blocks):
                    block = gram[(i - j) * cols : (i - j + 1) * cols]
                    barred = pen[m, i * cols : (i + 1) * cols, :]
                    down = block + jnp.concatenate([barred] * (cols // LANES), axis=1)
                    if i == j:
                        a = lax.broadcasted_iota(jnp.int32, (cols, cols), 0)
                        b = lax.broadcasted_iota(jnp.int32, (cols, cols), 1)
                        down = jnp.where(a == b, BARRED, down)
                    best = jnp.maximum(best, jnp.max(down, axis=0, keepdims=True))
                    if i > j:
                        side = block + barred_cols[:, j * cols : (j + 1) * cols]
                        for k in range(cols // LANES):
                            piece = side[:, k * LANES : (k + 1) * LANES]
                            across[i] = piece if across[i] is None else jnp.maximum(across[i], piece)
                if across[j] is not None:
                    best = jnp.maximum(best, jnp.max(across[j].T, axis=0, keepdims=True))
                val_ref[2 * m : 2 * m + 1, j * cols : (j + 1) * cols] = best

    values = 2 * members
    tiles = per_member // LANES
    stacked = [val_ref[:, i * LANES : (i + 1) * LANES] for i in range(tiles)]
    turned[...] = jnp.concatenate(stacked + [jnp.zeros((LANES - tiles * values, LANES), F32)], axis=0).T
    span = LANES // slot_size
    held_rows = [turned[pl.ds(k, span, stride=slot_size), :] for k in range(slot_size)]
    group = lax.broadcasted_iota(jnp.int32, (span, LANES), 1) // values
    bit = 1
    while bit < slot_size:
        odd = (group & bit) != 0
        for k in range(slot_size):
            if not k & bit:
                low, high = held_rows[k], held_rows[k | bit]
                held_rows[k] = jnp.where(odd, pltpu.roll(high, bit * values, axis=1), low)
                held_rows[k | bit] = jnp.where(odd, high, pltpu.roll(low, LANES - bit * values, axis=1))
        bit *= 2
    for i in range(tiles):
        back_ref[i * span : (i + 1) * span, :] = held_rows[i]


def compare(arrived, members, slot_size):
    slots, feats = arrived.shape
    per_member = slots // members
    sources = per_member // slot_size
    vmem = pl.BlockSpec(memory_space=pltpu.VMEM)
    return pl.pallas_call(
        functools.partial(compare_kernel, members, slot_size),
        in_specs=[vmem],
        out_specs=[vmem, vmem],
        out_shape=[
            jax.ShapeDtypeStruct((members, feats), F32),
            pltpu.VMEM((sources, LANES), F32),
        ],
        scratch_shapes=[
            pltpu.VMEM((members, per_member + 16, feats), BF16),
            pltpu.VMEM((members, per_member, LANES), F32),
            pltpu.VMEM((2 * members, per_member), F32),
            pltpu.VMEM((LANES, LANES), F32),
        ],
        compiler_params=pltpu.CompilerParams(vmem_limit_bytes=40 * 1024 * 1024),
        name="compare",
    )(pltpu.with_memory_space_constraint(arrived.reshape(sources, members * slot_size, feats), pltpu.VMEM))


def pick_kernel(members, slot_size, back_ref, flat_ref, max_ref, cos_ref, turned):
    owners = back_ref.shape[0]
    rows = flat_ref.shape[1]
    each = 2 * slot_size
    turned[...] = back_ref[...].T
    wide = jnp.concatenate(
        [
            jnp.concatenate(
                [turned[pl.ds(2 * m + v, slot_size, stride=2 * members), :] for v in range(2)], axis=0
            )
            for m in range(members)
        ],
        axis=1,
    )
    high = wide.astype(BF16)
    left = wide - high.astype(F32)
    mid = left.astype(BF16)
    low = (left - mid.astype(F32)).astype(BF16)
    pieces = jnp.concatenate([high, mid, low], axis=0)
    cols = 512
    owner = lax.broadcasted_iota(jnp.int32, (owners, cols), 0) * members
    for b in range(rows // cols):
        at = slice(b * cols, (b + 1) * cols)
        flat = flat_ref[:, at]
        group = lax.div(flat, slot_size)
        rank = lax.rem(flat, slot_size)
        hits = jnp.concatenate(
            [jnp.where(owner == group - m, 1.0, 0.0).astype(BF16) for m in range(members)], axis=0
        )
        got = jnp.dot(pieces, hits, preferred_element_type=F32)
        got = got[:each] + got[each : 2 * each] + got[2 * each :]
        mine = lax.broadcasted_iota(jnp.int32, (slot_size, cols), 0) == rank
        max_ref[:, at] = jnp.sum(jnp.where(mine, got[:slot_size], 0.0), axis=0, keepdims=True)
        cos_ref[:, at] = jnp.sum(jnp.where(mine, got[slot_size:], 0.0), axis=0, keepdims=True)


def pick(back, flat, members, slot_size):
    rows = flat.shape[1]
    return pl.pallas_call(
        functools.partial(pick_kernel, members, slot_size),
        out_shape=[jax.ShapeDtypeStruct((1, rows), F32)] * 2,
        scratch_shapes=[pltpu.VMEM((back.shape[1], back.shape[0]), F32)],
        compiler_params=pltpu.CompilerParams(vmem_limit_bytes=32 * 1024 * 1024),
        name="pick",
    )(back, flat)


def on_device(embeddings, assignment, cluster_order):
    devices = lax.axis_size("dp") * lax.axis_size("sub")
    rows, feats = embeddings.shape
    clusters = cluster_order.shape[0]
    members = clusters // devices
    slot_size = 2 * rows // clusters
    both = ("dp", "sub")
    outgoing, flat = place(
        assignment.reshape(1, rows), cluster_order.reshape(1, clusters), embeddings, slot_size
    )
    arrived = lax.all_to_all(
        outgoing.reshape(devices, members * slot_size, feats), both, split_axis=0, concat_axis=0, tiled=True
    )
    centers, values = compare(arrived.reshape(clusters * slot_size, feats), members, slot_size)
    back = lax.all_to_all(
        values.reshape(devices, 1, values.shape[1]), both, split_axis=0, concat_axis=0, tiled=True
    ).reshape(values.shape)
    row_max, center_cos = pick(back, flat, members, slot_size)
    return centers, row_max.reshape(rows), center_cos.reshape(rows)


def solution(mesh):
    return jax.shard_map(
        on_device,
        mesh=mesh,
        in_specs=(P(("dp", "sub"), None), P(("dp", "sub"), None), P()),
        out_specs=(P(("dp", "sub"), None), P(("dp", "sub")), P(("dp", "sub"))),
        check_vma=False,
    )
```
